32 devices in a mesh: chain: 4 (over z), rows: 8 (over y, x, core).
Axes of the slice: x: 2, y: 2, z: 4, core: 2. Of those that a mesh axis runs over, the one named last changes fastest.
Arguments:
- right_side: bfloat16 [8192, 768], P(('chain', 'rows')), may hold values from -6 to 6
- entering: float32 [8192, 256], P(('chain', 'rows')), may hold values from -6 to 6
- first_updates: float32 [2048, 512], P('rows'), may hold values from -6 to 6
- diag_inverse: bfloat16 [4, 2048, 2048], P('chain', 'rows'), may hold values from -2 to 2, as said below
- tile_blocks: bfloat16 [4, 8, 128, 2048], P('chain', 'rows'), may hold values from -0.1875 to 0.1875
- target_row_blocks: int32 [4, 8], P('chain', 'rows'), may hold values from 0 to 15
- tile_usage_order: int32 [4, 8], P('chain'), may hold values from 0 to 7, each once within a row
- live_tile_count: int32 [4], P('chain'), may hold values from 2 to 8
Outputs:
- solution: float32 [8192, 768], P(('chain', 'rows'))
- updates: float32 [8192, 768], P(('chain', 'rows'))
The draws below stay inside these ranges and needn't reach their ends.
Inputs may be any that keep to these rules, and one draw needn't show every extreme that they name: `diag_inverse`: lower triangular. `tile_usage_order`: each row names each of the 8 slots once; the first live_tile_count[s] entries name the live slots of supernode s.
All inputs are finite; a program needn't handle non-finite values.
Results may differ from the reference program's by a relative error of at most 0.013.
Values may be sent and summed in bfloat16 or wider, within the bound.
No kernel may reach another device: no remote copies, remote signals or barrier semaphores. Data moves between devices by JAX's collectives and lax.ppermute only.
A program may use at most 64 MiB of HBM per device.

```python
import math
import jax
import jax.numpy as jnp
from jax import lax

W = 2048
TILE = 128
PW = 256
TICKS = 3
TPD = 1
NS = 4
TT = 8
NB = 16
ORDER = 8192
N_ROWS = 8


def draw_diag_inverse(key, part):
    first_key, second_key = jax.random.split(jax.random.fold_in(key, 17))
    scales = jax.random.uniform(first_key, (NS, W, 1), jnp.float32, 0.5, 1.5)
    lower = jax.random.normal(second_key, (NS, W, W), jnp.float32) * (0.8 / math.sqrt(W))
    row_index = lax.broadcasted_iota(jnp.int32, (W, W), 0)
    col_index = lax.broadcasted_iota(jnp.int32, (W, W), 1)
    below = (col_index < row_index).astype(jnp.float32)
    diagonal_mask = (col_index == row_index).astype(jnp.float32)
    return (lower * below[None] + scales * diagonal_mask[None]).astype(jnp.bfloat16)


def place_ends(values, stream_key, smallest, top_value):
    longest = values.shape.index(max(values.shape))
    spots = []
    for shift in (0, 1):
        where = [jax.random.randint(jax.random.fold_in(stream_key, axis), (), 0, length) for axis, length in enumerate(values.shape)]
        where[longest] = (where[longest] + shift) % values.shape[longest]
        spots.append(tuple(where))
    return values.at[spots[0]].set(smallest).at[spots[1]].set(top_value)


def steps_of(own_key, dims, cuts, smallest, top_value):
    factor_of = 1.0
    for dim, blocks in cuts:
        steps = jax.random.uniform(jax.random.fold_in(jax.random.fold_in(own_key, 6), dim), (blocks,), jnp.float32, smallest / len(cuts), top_value / len(cuts))
        factor_of = factor_of * jnp.repeat(jnp.exp(steps), dims[dim] // blocks).reshape((-1,) + (1,) * (len(dims) - 1 - dim))
    return factor_of


def noise(key, dims, width, limit, cuts=(), kind=jnp.bfloat16):
    level = steps_of(key, dims, cuts, -0.22, 0.18) if cuts else 1.0
    drawn = jax.random.normal(key, dims, jnp.float32) * width * level
    return jnp.minimum(jnp.maximum(drawn, -limit), limit).astype(kind)


def setup_inputs(seed: int = 0) -> dict:
    key_of = jax.random.split(jax.random.key(seed), 9)
    return {
        "right_side": noise(key_of[0], (ORDER, TICKS * PW), 1.0, 6.0, ((0, 32),)),
        "entering": noise(key_of[1], (ORDER, PW), 1.0, 6.0, ((0, 32),), jnp.float32),
        "first_updates": noise(key_of[2], (W, (TICKS - 1) * PW), 1.0, 6.0, ((0, 8),), jnp.float32),
        "diag_inverse": draw_diag_inverse(jax.random.fold_in(key_of[8], 71), 0),
        "tile_blocks": noise(key_of[4], (NS, TT, TILE, W), (W * TT // NB) ** -0.5, 0.1875, ((0, 4), (1, 8))),
        "target_row_blocks": place_ends(jax.random.randint(key_of[5], (NS, TT), 0, NB), jax.random.fold_in(key_of[5], 1), 0, NB - 1).astype(jnp.int32),
        "tile_usage_order": jax.vmap(lambda own: jax.random.permutation(own, TT))(jax.random.split(key_of[6], NS)).reshape((NS, TT)).astype(jnp.int32),
        "live_tile_count": place_ends(jax.random.randint(key_of[7], (NS,), TT // 4, TT + 1), jax.random.fold_in(key_of[7], 1), TT // 4, TT).astype(jnp.int32),
    }


def supernode_work(head_rows, inverse_block, tiles, targets, order_row, live_count):
    every_slot = order_row.shape[0]
    positions = jnp.arange(every_slot, dtype=jnp.int32)
    block_index = jnp.arange(NB, dtype=jnp.int32)
    solved = jnp.dot(inverse_block, head_rows, preferred_element_type=jnp.float32)
    counted = positions < live_count
    matches = jnp.logical_and(order_row[None, :] == positions[:, None], counted[None, :])
    alive = jnp.sum(matches.astype(jnp.float32), axis=1)
    placing = (block_index[:, None] == targets[None, :]).astype(jnp.float32) * alive[None, :]
    device_tiles = tiles.reshape(N_ROWS, TPD, TILE, W)
    device_placing = jnp.transpose(placing.reshape(NB, N_ROWS, TPD), (1, 0, 2))
    head_wide = head_rows.astype(jnp.float32)

    def add_device(running, members):
        own_tiles, own_placing = members
        products = jnp.einsum("mtw,wp->mtp", own_tiles.astype(jnp.float32), head_wide, precision=lax.Precision.HIGHEST)
        partial_value = jnp.einsum("bm,mtp->btp", own_placing, products, precision=lax.Precision.HIGHEST).reshape(W, -1)
        rounded = lax.optimization_barrier(partial_value.astype(jnp.bfloat16))
        return running + rounded.astype(jnp.float32), None

    starting = jnp.zeros((W, head_rows.shape[1]), jnp.float32)
    handed, _ = lax.scan(add_device, starting, (device_tiles, device_placing))
    return solved, handed


def reference(right_side, entering, first_updates, diag_inverse, tile_blocks, target_row_blocks, tile_usage_order, live_tile_count):
    solved_cols = [[] for s in range(NS)]
    handed_cols = [[] for s in range(NS)]
    for tick in range(TICKS):
        for supernode in range(NS):
            if tick == 0:
                incoming = entering[supernode * W:(supernode + 1) * W]
            elif supernode == 0:
                incoming = first_updates[:, (tick - 1) * PW:tick * PW]
            else:
                incoming = handed_cols[supernode - 1][tick - 1]
            given_rows = right_side[supernode * W:(supernode + 1) * W, tick * PW:(tick + 1) * PW]
            head_rows = (given_rows.astype(jnp.float32) - incoming).astype(jnp.bfloat16)
            solved, handed = supernode_work(head_rows, diag_inverse[supernode], tile_blocks[supernode], target_row_blocks[supernode], tile_usage_order[supernode], live_tile_count[supernode])
            solved_cols[supernode].append(solved)
            handed_cols[supernode].append(handed)
    solution = jnp.concatenate([jnp.concatenate(solved_cols[s], axis=1) for s in range(NS)], axis=0)
    updates = jnp.concatenate([jnp.concatenate(handed_cols[s], axis=1) for s in range(NS)], axis=0)
    return solution, updates
```

```python
import functools

import jax
import jax.numpy as jnp
from jax import lax
from jax.experimental import pallas as pl
from jax.experimental.pallas import tpu as pltpu
from jax.sharding import PartitionSpec as P

PW = 256
NOTE = 16
CORES = 2
WIDE = jnp.float32
NARROW = jnp.bfloat16


def partner(chip, offset, chips):
    if chips & (chips - 1) == 0:
        return chip ^ offset
    return (chip + offset) % chips


def multiply(matrix, vector):
    return jnp.dot(matrix, vector, preferred_element_type=WIDE)


def hop(block, offset_of, step, ends):
    chips, chain = ends
    route = []
    for stage in range(chain - step):
        for chip in range(chips):
            for core in range(CORES):
                goal = partner(chip, offset_of(core), chips)
                source = (stage * chips + chip) * CORES + core
                target = ((stage + step) * chips + goal) * CORES + core
                route.append((source, target))
    return lax.ppermute(block, ("chain", "rows"), route)


def swap(block, rows):
    return lax.ppermute(block, "rows", [(i, i ^ 1) for i in range(rows)])


def place():
    me = lax.axis_index("rows")
    return me, lax.div(me, CORES), lax.rem(me, CORES)


def source_row(index, chips):
    _, chip, core = place()
    offset, side = divmod(index, CORES)
    other = partner(chip, (chips - offset) % chips if chips & (chips - 1) else offset, chips)
    return other * CORES + (core if side == 0 else 1 - core)


def lay_out(whole, columns, pieces, chips):
    height = pieces[0].shape[0]
    for index, piece in enumerate(pieces):
        row = source_row(index, chips)
        whole[pl.ds(pl.multiple_of(row * height, height), height), columns] = piece[...]


def is_live(order, count, slot):
    found = jnp.int32(0)
    for k in range(order.shape[1]):
        hit = jnp.logical_and(order[0, k] == slot, k < count[0])
        found = jnp.where(hit, jnp.int32(1), found)
    return found


def write_tiles(out, products, targets, order, count, slots, tile):
    me, _, core = place()
    for side in range(CORES):
        row = me if side == 0 else me + 1 - 2 * core
        for slot in range(slots):
            base = (side * slots + slot) * (tile + NOTE)
            live = is_live(order, count, row * slots + slot)
            product = products[(side * slots + slot) * tile : (side * slots + slot + 1) * tile]
            out[base : base + tile] = jnp.where(live > 0, product, 0.0).astype(NARROW)
            note = jnp.full((NOTE, PW), targets[side][0, slot], jnp.int32)
            out[base + tile : base + tile + NOTE] = note.astype(WIDE).astype(NARROW)


def read_targets(sent, tile):
    found = []
    for index in range(sent.shape[0] // (tile + NOTE)):
        base = index * (tile + NOTE) + tile
        note = sent[base : base + NOTE, 0:128].astype(WIDE).astype(jnp.int32)
        found.append(note[0, 0])
    return found


def read_tiles(sent, tile):
    count = sent.shape[0] // (tile + NOTE)
    return jnp.concatenate(
        [sent[i * (tile + NOTE) : i * (tile + NOTE) + tile] for i in range(count)], axis=0
    )


def spread(matrices, sent, tile):
    targets = read_targets(sent, tile)
    picked = [
        jnp.concatenate(
            [m[:, pl.ds(pl.multiple_of(t * tile, tile), tile)] for t in targets], axis=1
        )
        for m in matrices
    ]
    return multiply(jnp.concatenate(picked, axis=0), read_tiles(sent, tile))


def first_kernel(chips, slots, tile, *refs):
    own, mate, own_target, mate_target, order, count = refs[:6]
    pieces, out, whole = refs[6:-2], refs[-2], refs[-1]
    lay_out(whole, slice(0, PW), pieces, chips)
    tiles = jnp.concatenate([own[...], mate[...]], axis=0)
    products = multiply(tiles, whole[...])
    write_tiles(out, products, (own_target, mate_target), order, count, slots, tile)


def ahead_kernel(chips, *refs):
    own, mate = refs[:2]
    pieces, out, whole = refs[2:-2], refs[-2], refs[-1]
    lay_out(whole, slice(0, whole.shape[1]), pieces, chips)
    tiles = jnp.concatenate([own[...], mate[...]], axis=0)
    out[...] = multiply(tiles, whole[...])


def next_kernel(tick, slots, tile, *refs):
    own, mate, own_target, mate_target, order, count, ahead = refs[:7]
    sent, out = refs[7:-1], refs[-1]
    products = ahead[:, (tick - 1) * PW : tick * PW]
    for one in sent:
        products = products - spread((own, mate), one, tile)
    write_tiles(out, products, (own_target, mate_target), order, count, slots, tile)


def solve_kernel(chips, tile, ticks, *refs):
    inverse = refs[0]
    parts = CORES * chips
    first, later = refs[1 : 1 + parts], refs[1 + parts : 1 + 2 * parts]
    sent, out, whole = refs[1 + 2 * parts : -2], refs[-2], refs[-1]
    lay_out(whole, slice(0, PW), first, chips)
    lay_out(whole, slice(PW, ticks * PW), later, chips)
    for tick in range(ticks):
        columns = slice(tick * PW, (tick + 1) * PW)
        solved = multiply(inverse[...], whole[:, columns])
        if tick:
            for one in sent[(tick - 1) * chips : tick * chips]:
                solved = solved - spread((inverse,), one, tile)
        out[:, columns] = solved


def update_kernel(chips, tile, ticks, *refs):
    sent, out = refs[:-1], refs[-1]
    height = out.shape[0]
    me, _, _ = place()
    out[...] = jnp.zeros(out.shape, out.dtype)
    for tick in range(ticks):
        columns = slice(tick * PW, (tick + 1) * PW)
        for one in sent[tick * chips : (tick + 1) * chips]:
            for index, target in enumerate(read_targets(one, tile)):
                base = index * (tile + NOTE)
                if height >= tile:
                    held = height // tile
                    spot = target - me * held

                    @pl.when(jnp.logical_and(spot >= 0, spot < held))
                    def _(one=one, base=base, spot=spot, columns=columns):
                        rows = pl.ds(pl.multiple_of(spot * tile, tile), tile)
                        out[rows, columns] += one[base : base + tile].astype(WIDE)

                else:
                    shares = tile // height
                    start = base + lax.rem(me, shares) * height

                    @pl.when(target == lax.div(me, shares))
                    def _(one=one, start=start, columns=columns):
                        rows = pl.ds(pl.multiple_of(start, NOTE), height)
                        out[:, columns] += one[rows].astype(WIDE)


def call(kernel, out_shape, args, scratch=(), flops=0):
    in_specs = [
        pl.BlockSpec(memory_space=pltpu.SMEM if a.dtype == jnp.int32 else pltpu.VMEM)
        for a in args
    ]
    moved = sum(a.size * a.dtype.itemsize for a in args)
    return pl.pallas_call(
        kernel,
        out_shape=out_shape,
        in_specs=in_specs,
        out_specs=pl.BlockSpec(memory_space=pltpu.VMEM),
        scratch_shapes=list(scratch),
        compiler_params=pltpu.CompilerParams(vmem_limit_bytes=40 * 1024 * 1024),
        cost_estimate=pl.CostEstimate(flops=flops, bytes_accessed=moved, transcendentals=0),
    )(*args)


def body(
    right_side,
    entering,
    first_updates,
    diag_inverse,
    tile_blocks,
    target_row_blocks,
    tile_usage_order,
    live_tile_count,
):
    rows, chain = lax.axis_size("rows"), lax.axis_size("chain")
    chips = rows // CORES
    slots, tile, separator = tile_blocks.shape[1:]
    height = right_side.shape[0]
    ticks = right_side.shape[1] // PW
    is_first = (lax.axis_index("chain") == 0).astype(WIDE)
    inverse = diag_inverse[0]
    own = tile_blocks[0].reshape(slots * tile, separator)
    ends = (chips, chain)

    def gather(block):
        pieces = [block, swap(block, rows)]
        for offset in range(1, chips):
            came = hop(block, lambda core, offset=offset: offset, 0, ends)
            pieces += [came, swap(came, rows)]
        return pieces

    def pass_on(block):
        half, found = chips // 2, []
        for i in range(half):
            came = hop(block, lambda core, i=i: core * half + i, 1, ends)
            found += [came, swap(came, rows)]
        return found

    def share(block):
        found = [block]
        offset = 1
        while offset < chips:
            if offset + 1 < chips:
                came = hop(block, lambda core, offset=offset: offset + core, 0, ends)
                found += [came, swap(came, rows)]
                offset += 2
            else:
                found.append(hop(block, lambda core, offset=offset: offset, 0, ends))
                offset += 1
        return found

    mate = swap(own, rows)
    mate_target = swap(target_row_blocks, rows)
    lists = (target_row_blocks, mate_target, tile_usage_order, live_tile_count)
    head = (right_side[:, :PW].astype(WIDE) - entering).astype(NARROW)
    later = (right_side[:, PW:].astype(WIDE) - is_first * first_updates).astype(NARROW)
    heads = gather(head)
    laters = gather(later)
    block_shape = jax.ShapeDtypeStruct((CORES * slots * (tile + NOTE), PW), NARROW)
    tile_rows = CORES * slots * tile
    work = 2 * tile_rows * separator * PW
    product = call(
        functools.partial(first_kernel, chips, slots, tile),
        block_shape,
        (own, mate, *lists, *heads),
        [pltpu.VMEM((separator, PW), NARROW)],
        work,
    )
    ahead = call(
        functools.partial(ahead_kernel, chips),
        jax.ShapeDtypeStruct((tile_rows, (ticks - 1) * PW), WIDE),
        (own, mate, *laters),
        [pltpu.VMEM((separator, (ticks - 1) * PW), NARROW)],
        work * (ticks - 1),
    )
    shared, came = [], []
    for tick in range(ticks):
        shared += share(product)
        if tick + 1 < ticks:
            sent = pass_on(product)
            came += sent
            product = call(
                functools.partial(next_kernel, tick + 1, slots, tile),
                block_shape,
                (own, mate, *lists, ahead, *sent),
                (),
                work // 2,
            )
    out_shape = jax.ShapeDtypeStruct((height, ticks * PW), WIDE)
    solved = call(
        functools.partial(solve_kernel, chips, tile, ticks),
        out_shape,
        (inverse, *heads, *laters, *came),
        [pltpu.VMEM((separator, ticks * PW), NARROW)],
        2 * height * separator * ticks * PW,
    )
    passed = call(
        functools.partial(update_kernel, chips, tile, ticks),
        out_shape,
        tuple(shared),
        (),
        height * ticks * PW,
    )
    return solved, passed


def solution(mesh):
    placed = (
        P(("chain", "rows"), None),
        P(("chain", "rows"), None),
        P("rows", None),
        P("chain", "rows", None),
        P("chain", "rows", None, None),
        P("chain", "rows"),
        P("chain", None),
        P("chain"),
    )
    return jax.shard_map(
        body,
        mesh=mesh,
        in_specs=placed,
        out_specs=(P(("chain", "rows"), None), P(("chain", "rows"), None)),
        check_vma=False,
    )
```

```python
import functools

import jax
import jax.numpy as jnp
from jax import lax
from jax.experimental import pallas as pl
from jax.experimental.pallas import tpu as pltpu
from jax.sharding import PartitionSpec as P

PW = 256
NOTE = 16
CORES = 2
WIDE = jnp.float32
NARROW = jnp.bfloat16


def partner(chip, offset, chips):
    if chips & (chips - 1) == 0:
        return chip ^ offset
    return (chip + offset) % chips


def multiply(matrix, vector):
    return jnp.dot(matrix, vector, preferred_element_type=WIDE)


def after(value, *others):
    return lax.optimization_barrier((value, *others))[0]


def hop(block, offset_of, step, ends):
    chips, chain = ends
    route = []
    for stage in range(chain - step):
        for chip in range(chips):
            for core in range(CORES):
                goal = partner(chip, offset_of(core), chips)
                source = (stage * chips + chip) * CORES + core
                target = ((stage + step) * chips + goal) * CORES + core
                route.append((source, target))
    return lax.ppermute(block, ("chain", "rows"), route)


def swap(block, rows):
    return lax.ppermute(block, "rows", [(i, i ^ 1) for i in range(rows)])


def place():
    me = lax.axis_index("rows")
    return me, lax.div(me, CORES), lax.rem(me, CORES)


def source_row(index, chips):
    _, chip, core = place()
    offset, side = divmod(index, CORES)
    other = partner(chip, (chips - offset) % chips if chips & (chips - 1) else offset, chips)
    return other * CORES + (core if side == 0 else 1 - core)


def lay_pairs(whole, columns, pieces, chips):
    height = pieces[0].shape[0] // CORES
    for offset, piece in enumerate(pieces):
        for side in range(CORES):
            row = source_row(offset * CORES + side, chips)
            rows = pl.ds(pl.multiple_of(row * height, height), height)
            whole[rows, columns] = piece[side * height : (side + 1) * height]


def is_live(order, count, slot):
    found = jnp.int32(0)
    for k in range(order.shape[1]):
        hit = jnp.logical_and(order[0, k] == slot, k < count[0])
        found = jnp.where(hit, jnp.int32(1), found)
    return found


def mark_kernel(slots, own_target, mate_target, order, count, notes, alive):
    me, _, core = place()
    for side, targets in enumerate((own_target, mate_target)):
        row = me if side == 0 else me + 1 - 2 * core
        for slot in range(slots):
            index = side * slots + slot
            rows = slice(index * NOTE, (index + 1) * NOTE)
            note = jnp.full((NOTE, notes.shape[1]), targets[0, slot], jnp.int32)
            notes[rows] = note.astype(WIDE).astype(NARROW)
            live = is_live(order, count, row * slots + slot)
            alive[index : index + 1] = jnp.full((1, notes.shape[1]), live).astype(WIDE)


def write_tiles(out, products, notes, alive, tile):
    for index in range(products.shape[0] // tile):
        base = index * (tile + NOTE)
        product = products[index * tile : (index + 1) * tile]
        kept = jnp.where(alive[index : index + 1] > 0, product, 0.0)
        out[base : base + tile] = kept.astype(NARROW)
        out[base + tile : base + tile + NOTE] = notes[index * NOTE : (index + 1) * NOTE]


def read_targets(sent, tile):
    found = []
    for index in range(sent.shape[0] // (tile + NOTE)):
        base = index * (tile + NOTE) + tile
        note = sent[base : base + NOTE, 0:128].astype(WIDE).astype(jnp.int32)
        found.append(note[0, 0])
    return found


def read_tiles(sent, tile):
    count = sent.shape[0] // (tile + NOTE)
    return jnp.concatenate(
        [sent[i * (tile + NOTE) : i * (tile + NOTE) + tile] for i in range(count)], axis=0
    )


def spread(matrices, sent, tile):
    targets = [t for one in sent for t in read_targets(one, tile)]
    picked = [
        jnp.concatenate(
            [m[:, pl.ds(pl.multiple_of(t * tile, tile), tile)] for t in targets], axis=1
        )
        for m in matrices
    ]
    tiles = jnp.concatenate([read_tiles(one, tile) for one in sent], axis=0)
    return multiply(jnp.concatenate(picked, axis=0), tiles)


def pair_kernel(panels, own, mate, out):
    half = out.shape[1] // panels
    height = own.shape[0] // panels
    for side, block in enumerate((own, mate)):
        rows = slice(side * height, (side + 1) * height)
        for panel in range(panels):
            columns = slice(panel * half, (panel + 1) * half)
            out[rows, columns] = block[panel * height : (panel + 1) * height]


def first_kernel(chips, tile, *refs):
    own, mate, notes, alive = refs[:4]
    pieces, out, whole = refs[4:-2], refs[-2], refs[-1]
    lay_pairs(whole, slice(0, whole.shape[1]), pieces, chips)
    tiles = jnp.concatenate([own[...], mate[...]], axis=0)
    products = multiply(tiles, whole[...])
    write_tiles(out, products, notes, alive, tile)


def ahead_kernel(chips, *refs):
    own, mate = refs[:2]
    pieces, out, whole = refs[2:-2], refs[-2], refs[-1]
    lay_pairs(whole, slice(0, whole.shape[1]), pieces, chips)
    tiles = jnp.concatenate([own[...], mate[...]], axis=0)
    out[...] = multiply(tiles, whole[...])


def next_kernel(chips, tick, tile, *refs):
    own, mate, notes, alive, ahead = refs[:5]
    sent, rest = refs[5 : 5 + chips], refs[5 + chips :]
    past, outs = rest[: len(rest) // 2], rest[len(rest) // 2 :]
    half = PW // CORES
    products = ahead[:, (tick - 1) * half : tick * half]
    products = products - spread((own, mate), sent, tile)
    out = outs[0]
    write_tiles(out, products, notes, alive, tile)
    for index, one in enumerate([*past, out] if past else []):
        history = outs[1]
        history[index * out.shape[0] : (index + 1) * out.shape[0]] = one[...]


def solve_kernel(chips, tile, ticks, *refs):
    inverse, mate = refs[:2]
    first, later = refs[2 : 2 + chips], refs[2 + chips : 2 + 2 * chips]
    sent, (out, other, whole) = refs[2 + 2 * chips : -3], refs[-3:]
    half = PW // CORES
    height = out.shape[0]
    lay_pairs(whole, slice(0, half), first, chips)
    lay_pairs(whole, slice(half, ticks * half), later, chips)
    matrix = jnp.concatenate([inverse[...], mate[...]], axis=0)
    solved = multiply(matrix, whole[...])
    for tick in range(ticks):
        columns = slice(tick * half, (tick + 1) * half)
        one_tick = solved[:, columns]
        if tick:
            here = sent[(tick - 1) * chips : tick * chips]
            one_tick = one_tick - spread((inverse, mate), here, tile)
        out[:, columns] = one_tick[:height]
        other[:, columns] = one_tick[height:].astype(other.dtype)


def update_kernel(tile, ticks, *refs):
    sent, (out, other, total) = refs[:-3], refs[-3:]
    half = PW // CORES
    height = out.shape[0]
    _, chip, core = place()
    size = total.shape[0]
    total[...] = jnp.zeros(total.shape, total.dtype)
    for one in sent:
        count = one.shape[0] // (tile + NOTE) // ticks
        for index, target in enumerate(read_targets(one, tile)):
            tick = index // count
            columns = slice(tick * half, (tick + 1) * half)
            base = index * (tile + NOTE)
            if size >= tile:
                held = size // tile
                spot = target - chip * held

                @pl.when(jnp.logical_and(spot >= 0, spot < held))
                def _(one=one, base=base, spot=spot, columns=columns):
                    rows = pl.ds(pl.multiple_of(spot * tile, tile), tile)
                    total[rows, columns] += one[base : base + tile].astype(WIDE)

            else:
                shares = tile // size
                start = base + lax.rem(chip, shares) * size

                @pl.when(target == lax.div(chip, shares))
                def _(one=one, start=start, columns=columns):
                    rows = pl.ds(pl.multiple_of(start, NOTE), size)
                    total[:, columns] += one[rows].astype(WIDE)

    out[...] = total[pl.ds(pl.multiple_of(core * height, height), height)]
    rest = total[pl.ds(pl.multiple_of((1 - core) * height, height), height)]
    other[...] = rest.astype(other.dtype)


def join_kernel(*refs):
    half = PW // CORES
    _, _, core = place()
    out, tick = refs[-1], 0
    for own, mate in zip(refs[0:-1:2], refs[1:-1:2]):
        for index in range(own.shape[1] // half):
            columns = slice(index * half, (index + 1) * half)
            for side, block in ((core, own), (1 - core, mate)):
                start = pl.multiple_of(tick * PW + side * half, half)
                out[:, pl.ds(start, half)] = block[:, columns].astype(out.dtype)
            tick += 1


def call(kernel, out_shape, args, scratch=()):
    in_specs = [
        pl.BlockSpec(memory_space=pltpu.SMEM if a.dtype == jnp.int32 else pltpu.VMEM)
        for a in args
    ]
    return pl.pallas_call(
        kernel,
        out_shape=out_shape,
        in_specs=in_specs,
        out_specs=jax.tree.map(lambda _: pl.BlockSpec(memory_space=pltpu.VMEM), out_shape),
        scratch_shapes=list(scratch),
        compiler_params=pltpu.CompilerParams(vmem_limit_bytes=40 * 1024 * 1024),
        cost_estimate=pl.CostEstimate(flops=1, bytes_accessed=1, transcendentals=0),
    )(*args)


def body(
    right_side,
    entering,
    first_updates,
    diag_inverse,
    tile_blocks,
    target_row_blocks,
    tile_usage_order,
    live_tile_count,
):
    rows, chain = lax.axis_size("rows"), lax.axis_size("chain")
    chips = rows // CORES
    slots, tile, separator = tile_blocks.shape[1:]
    height = right_side.shape[0]
    ticks = right_side.shape[1] // PW
    half = PW // CORES
    inverse = diag_inverse[0]
    own = tile_blocks[0].reshape(slots * tile, separator)
    ends = (chips, chain)

    def around(block):
        return [
            hop(block, lambda core, offset=offset: offset, 0, ends) for offset in range(1, chips)
        ]

    def shape(height, width, kind):
        return jax.ShapeDtypeStruct((height, width), kind)

    is_low = lax.rem(lax.axis_index("rows"), CORES) == 0
    is_first = (lax.axis_index("chain") == 0).astype(WIDE)

    def pair_up(panels, *others):
        count = len(panels)
        split = [(one[:, :half], one[:, half:]) for one in panels]
        mine = jnp.concatenate([jnp.where(is_low, a, b) for a, b in split], axis=0)
        other = jnp.concatenate([jnp.where(is_low, b, a) for a, b in split], axis=0)
        return call(
            functools.partial(pair_kernel, count),
            shape(CORES * height, count * half, NARROW),
            (after(mine, *others) if others else mine, swap(other, rows)),
        )

    def panel(tick):
        return right_side[:, tick * PW : (tick + 1) * PW].astype(WIDE)

    head = pair_up([(panel(0) - entering).astype(NARROW)])
    heads = [head, *around(head)]
    mate = swap(own, rows)
    mate_target = swap(target_row_blocks, rows)
    marks = call(
        functools.partial(mark_kernel, slots),
        (
            shape(CORES * slots * NOTE, half, NARROW),
            shape(CORES * slots, half, WIDE),
        ),
        (target_row_blocks, mate_target, tile_usage_order, live_tile_count),
    )
    rest = [
        (panel(t) - is_first * first_updates[:, (t - 1) * PW : t * PW]).astype(NARROW)
        for t in range(1, ticks)
    ]
    rest = after(pair_up(rest, mate, marks[1]), *heads[1:])
    laters = [rest, *around(rest)]

    block_rows = CORES * slots * (tile + NOTE)
    block = shape(block_rows, half, NARROW)
    tile_rows = CORES * slots * tile
    product = call(
        functools.partial(first_kernel, chips, tile),
        block,
        (own, mate, *marks, *heads),
        [pltpu.VMEM((separator, half), NARROW)],
    )
    ahead, came, past, shared = None, [], [], []
    for tick in range(1, ticks):
        past.append(product)
        arrived = hop(product, lambda core: 0, 1, ends)
        sent = [arrived, *around(arrived)]
        came += sent
        if ahead is None:
            ahead = call(
                functools.partial(ahead_kernel, chips),
                shape(tile_rows, (ticks - 1) * half, WIDE),
                (own, mate, *[after(one, arrived) for one in laters]),
                [pltpu.VMEM((separator, (ticks - 1) * half), NARROW)],
            )
        earlier = past if tick == ticks - 2 else []
        history = shape((tick + 1) * block_rows, half, NARROW)
        product, *history = call(
            functools.partial(next_kernel, chips, tick, tile),
            (block, history) if earlier else (block,),
            (own, mate, *marks, ahead, *sent, *earlier),
        )
        if tick == ticks - 2:
            shared = [history[0], *around(history[0])]
    last = [product, *around(product)]
    mate_inverse = swap(after(inverse, past[-1]), rows)
    mine, other = call(
        functools.partial(solve_kernel, chips, tile, ticks),
        (shape(height, ticks * half, WIDE), shape(height, ticks * half, NARROW)),
        (inverse, mate_inverse, *heads, *laters, *came[:-1], after(came[-1], product)),
        [pltpu.VMEM((separator, ticks * half), NARROW)],
    )
    out = shape(height, ticks * PW, WIDE)
    solved = call(join_kernel, out, (mine, swap(other, rows)))

    def add_up(count, blocks, kind):
        mine, other = call(
            functools.partial(update_kernel, tile, count),
            (shape(height, count * half, WIDE), shape(height, count * half, kind)),
            tuple(blocks),
            [pltpu.VMEM((CORES * height, count * half), WIDE)],
        )
        return mine, swap(other, rows)

    passed = (
        *add_up(ticks - 1, [after(shared[0], product), *shared[1:]], NARROW),
        *add_up(1, last, WIDE),
    )
    passed = call(join_kernel, out, passed[:-1] + (after(passed[-1], solved),))
    return solved, passed


def solution(mesh):
    placed = (
        P(("chain", "rows"), None),
        P(("chain", "rows"), None),
        P("rows", None),
        P("chain", "rows", None),
        P("chain", "rows", None, None),
        P("chain", "rows"),
        P("chain", None),
        P("chain"),
    )
    return jax.shard_map(
        body,
        mesh=mesh,
        in_specs=placed,
        out_specs=(P(("chain", "rows"), None), P(("chain", "rows"), None)),
        check_vma=False,
    )
```

```python
import functools

import jax
import jax.numpy as jnp
from jax import lax
from jax.experimental import pallas as pl
from jax.experimental.pallas import tpu as pltpu
from jax.sharding import PartitionSpec as P

PW = 256
NOTE = 16
CORES = 2
WIDE = jnp.float32
NARROW = jnp.bfloat16


def partner(chip, offset, chips):
    if chips & (chips - 1) == 0:
        return chip ^ offset
    return (chip + offset) % chips


def multiply(matrix, vector):
    return jnp.dot(matrix, vector, preferred_element_type=WIDE)


def after(value, *others):
    return lax.optimization_barrier((value, *others))[0]


def hop(block, offset_of, step, ends):
    chips, chain = ends
    route = []
    for stage in range(chain - step):
        for chip in range(chips):
            for core in range(CORES):
                goal = partner(chip, offset_of(core), chips)
                source = (stage * chips + chip) * CORES + core
                target = ((stage + step) * chips + goal) * CORES + core
                route.append((source, target))
    return lax.ppermute(block, ("chain", "rows"), route)


def swap(block, rows):
    return lax.ppermute(block, "rows", [(i, i ^ 1) for i in range(rows)])


def place():
    me = lax.axis_index("rows")
    return me, lax.div(me, CORES), lax.rem(me, CORES)


def source_row(index, chips):
    _, chip, core = place()
    offset, side = divmod(index, CORES)
    other = partner(chip, (chips - offset) % chips if chips & (chips - 1) else offset, chips)
    return other * CORES + (core if side == 0 else 1 - core)


def lay_pairs(whole, columns, pieces, chips):
    height = pieces[0].shape[0] // CORES
    for offset, piece in enumerate(pieces):
        for side in range(CORES):
            row = source_row(offset * CORES + side, chips)
            rows = pl.ds(pl.multiple_of(row * height, height), height)
            whole[rows, columns] = piece[side * height : (side + 1) * height]


def is_live(order, count, slot):
    found = jnp.int32(0)
    for k in range(order.shape[1]):
        hit = jnp.logical_and(order[0, k] == slot, k < count[0])
        found = jnp.where(hit, jnp.int32(1), found)
    return found


def mark_kernel(slots, own_target, mate_target, order, count, notes, alive):
    me, _, core = place()
    for side, targets in enumerate((own_target, mate_target)):
        row = me if side == 0 else me + 1 - 2 * core
        for slot in range(slots):
            index = side * slots + slot
            rows = slice(index * NOTE, (index + 1) * NOTE)
            note = jnp.full((NOTE, notes.shape[1]), targets[0, slot], jnp.int32)
            notes[rows] = note.astype(WIDE).astype(NARROW)
            live = is_live(order, count, row * slots + slot)
            alive[index : index + 1] = jnp.full((1, notes.shape[1]), live).astype(WIDE)


def write_tiles(out, products, notes, alive, tile):
    rows = products.shape[0]
    for index in range(rows // tile):
        here = slice(index * tile, (index + 1) * tile)
        kept = jnp.where(alive[index : index + 1] > 0, products[here], 0.0)
        out[here] = kept.astype(NARROW)
    out[rows:] = notes[...]


def read_targets(sent, count):
    first = sent.shape[0] - count * NOTE
    found = []
    for index in range(count):
        note = sent[first + index * NOTE : first + (index + 1) * NOTE, 0:128]
        found.append(note.astype(WIDE).astype(jnp.int32)[0, 0])
    return found


def spread(matrices, sent, tile):
    count = sent[0].shape[0] // (tile + NOTE)
    targets = [t for one in sent for t in read_targets(one, count)]
    picked = [
        jnp.concatenate(
            [m[:, pl.ds(pl.multiple_of(t * tile, tile), tile)] for t in targets], axis=1
        )
        for m in matrices
    ]
    tiles = jnp.concatenate([one[: count * tile] for one in sent], axis=0)
    return multiply(jnp.concatenate(picked, axis=0), tiles)


def pair_kernel(panels, own, mate, out):
    half = out.shape[1] // panels
    height = own.shape[0] // panels
    for side, block in enumerate((own, mate)):
        rows = slice(side * height, (side + 1) * height)
        for panel in range(panels):
            columns = slice(panel * half, (panel + 1) * half)
            out[rows, columns] = block[panel * height : (panel + 1) * height]


def first_kernel(chips, tile, *refs):
    own, mate, notes, alive = refs[:4]
    pieces, out, whole = refs[4:-2], refs[-2], refs[-1]
    lay_pairs(whole, slice(0, whole.shape[1]), pieces, chips)
    tiles = jnp.concatenate([own[...], mate[...]], axis=0)
    products = multiply(tiles, whole[...])
    write_tiles(out, products, notes, alive, tile)


def ahead_kernel(chips, *refs):
    own, mate = refs[:2]
    pieces, out, whole = refs[2:-2], refs[-2], refs[-1]
    lay_pairs(whole, slice(0, whole.shape[1]), pieces, chips)
    tiles = jnp.concatenate([own[...], mate[...]], axis=0)
    out[...] = multiply(tiles, whole[...])


def next_kernel(chips, tick, tile, *refs):
    own, mate, notes, alive, ahead = refs[:5]
    sent, rest = refs[5 : 5 + chips], refs[5 + chips :]
    past, outs = rest[: len(rest) // 2], rest[len(rest) // 2 :]
    half = PW // CORES
    products = ahead[:, (tick - 1) * half : tick * half]
    products = products - spread((own, mate), sent, tile)
    out = outs[0]
    write_tiles(out, products, notes, alive, tile)
    rows = products.shape[0]
    for index, one in enumerate([*past, out] if past else []):
        outs[1][index * rows : (index + 1) * rows] = one[:rows]
    if past:
        outs[1][(len(past) + 1) * rows :] = notes[...]


def solve_kernel(chips, tile, ticks, *refs):
    inverse, mate = refs[:2]
    first, later = refs[2 : 2 + chips], refs[2 + chips : 2 + 2 * chips]
    sent, (out, other, whole) = refs[2 + 2 * chips : -3], refs[-3:]
    half = PW // CORES
    height = out.shape[0]
    lay_pairs(whole, slice(0, half), first, chips)
    lay_pairs(whole, slice(half, ticks * half), later, chips)
    matrix = jnp.concatenate([inverse[...], mate[...]], axis=0)
    solved = multiply(matrix, whole[...])
    for tick in range(ticks):
        columns = slice(tick * half, (tick + 1) * half)
        one_tick = solved[:, columns]
        if tick:
            here = sent[(tick - 1) * chips : tick * chips]
            one_tick = one_tick - spread((inverse, mate), here, tile)
        out[:, columns] = one_tick[:height]
        other[:, columns] = one_tick[height:].astype(other.dtype)


def update_kernel(tile, ticks, count, *refs):
    sent, (out, other, total) = refs[:-3], refs[-3:]
    half = PW // CORES
    height = out.shape[0]
    _, chip, core = place()
    size = total.shape[0]
    total[...] = jnp.zeros(total.shape, total.dtype)
    for one in sent:
        targets = read_targets(one, count)
        for index in range(ticks * count):
            tick, target = index // count, targets[index % count]
            columns = slice(tick * half, (tick + 1) * half)
            base = index * tile
            if size >= tile:
                held = size // tile
                spot = target - chip * held

                @pl.when(jnp.logical_and(spot >= 0, spot < held))
                def _(one=one, base=base, spot=spot, columns=columns):
                    rows = pl.ds(pl.multiple_of(spot * tile, tile), tile)
                    total[rows, columns] += one[base : base + tile].astype(WIDE)

            else:
                shares = tile // size
                start = base + lax.rem(chip, shares) * size

                @pl.when(target == lax.div(chip, shares))
                def _(one=one, start=start, columns=columns):
                    rows = pl.ds(pl.multiple_of(start, NOTE), size)
                    total[:, columns] += one[rows].astype(WIDE)

    out[...] = total[pl.ds(pl.multiple_of(core * height, height), height)]
    rest = total[pl.ds(pl.multiple_of((1 - core) * height, height), height)]
    other[...] = rest.astype(other.dtype)


def join_kernel(*refs):
    half = PW // CORES
    _, _, core = place()
    out, tick = refs[-1], 0
    for own, mate in zip(refs[0:-1:2], refs[1:-1:2]):
        for index in range(own.shape[1] // half):
            columns = slice(index * half, (index + 1) * half)
            for side, block in ((core, own), (1 - core, mate)):
                start = pl.multiple_of(tick * PW + side * half, half)
                out[:, pl.ds(start, half)] = block[:, columns].astype(out.dtype)
            tick += 1


def call(kernel, out_shape, args, scratch=(), moved=1):
    in_specs = [
        pl.BlockSpec(memory_space=pltpu.SMEM if a.dtype == jnp.int32 else pltpu.VMEM)
        for a in args
    ]
    return pl.pallas_call(
        kernel,
        out_shape=out_shape,
        in_specs=in_specs,
        out_specs=jax.tree.map(lambda _: pl.BlockSpec(memory_space=pltpu.VMEM), out_shape),
        scratch_shapes=list(scratch),
        compiler_params=pltpu.CompilerParams(vmem_limit_bytes=40 * 1024 * 1024),
        cost_estimate=pl.CostEstimate(flops=1, bytes_accessed=moved, transcendentals=0),
    )(*args)


def body(
    right_side,
    entering,
    first_updates,
    diag_inverse,
    tile_blocks,
    target_row_blocks,
    tile_usage_order,
    live_tile_count,
):
    rows, chain = lax.axis_size("rows"), lax.axis_size("chain")
    chips = rows // CORES
    slots, tile, separator = tile_blocks.shape[1:]
    height = right_side.shape[0]
    ticks = right_side.shape[1] // PW
    half = PW // CORES
    inverse = diag_inverse[0]
    own = tile_blocks[0].reshape(slots * tile, separator)
    ends = (chips, chain)

    def around(block):
        return [
            hop(block, lambda core, offset=offset: offset, 0, ends) for offset in range(1, chips)
        ]

    def shape(height, width, kind):
        return jax.ShapeDtypeStruct((height, width), kind)

    is_low = lax.rem(lax.axis_index("rows"), CORES) == 0
    is_first = (lax.axis_index("chain") == 0).astype(WIDE)

    def pair_up(panels, *others):
        count = len(panels)
        split = [(one[:, :half], one[:, half:]) for one in panels]
        mine = jnp.concatenate([jnp.where(is_low, a, b) for a, b in split], axis=0)
        other = jnp.concatenate([jnp.where(is_low, b, a) for a, b in split], axis=0)
        return call(
            functools.partial(pair_kernel, count),
            shape(CORES * height, count * half, NARROW),
            (after(mine, *others) if others else mine, swap(other, rows)),
        )

    def panel(tick):
        return right_side[:, tick * PW : (tick + 1) * PW].astype(WIDE)

    head = pair_up([(panel(0) - entering).astype(NARROW)])
    heads = [head, *around(head)]
    mate = swap(own, rows)
    mate_target = swap(target_row_blocks, rows)
    mate_inverse = swap(inverse, rows)
    marks = call(
        functools.partial(mark_kernel, slots),
        (
            shape(CORES * slots * NOTE, half, NARROW),
            shape(CORES * slots, half, WIDE),
        ),
        (target_row_blocks, mate_target, tile_usage_order, live_tile_count),
    )
    rest = [
        (panel(t) - is_first * first_updates[:, (t - 1) * PW : t * PW]).astype(NARROW)
        for t in range(1, ticks)
    ]
    rest = after(pair_up(rest, mate, mate_inverse, marks[1]), *heads[1:])
    laters = [rest, *around(rest)]

    block_rows = CORES * slots * (tile + NOTE)
    block = shape(block_rows, half, NARROW)
    tile_rows = CORES * slots * tile
    product = call(
        functools.partial(first_kernel, chips, tile),
        block,
        (own, mate, *marks, *heads),
        [pltpu.VMEM((separator, half), NARROW)],
    )
    ahead, came, past, shared = None, [], [], []
    for tick in range(1, ticks):
        past.append(product)
        arrived = hop(product, lambda core: 0, 1, ends)
        sent = [arrived, *around(arrived)]
        came += sent
        if ahead is None:
            ahead = call(
                functools.partial(ahead_kernel, chips),
                shape(tile_rows, (ticks - 1) * half, WIDE),
                (own, mate, *[after(one, arrived) for one in laters]),
                [pltpu.VMEM((separator, (ticks - 1) * half), NARROW)],
            )
        earlier = past if tick == ticks - 2 else []
        history = shape(block_rows + tick * tile_rows, half, NARROW)
        product, *history = call(
            functools.partial(next_kernel, chips, tick, tile),
            (block, history) if earlier else (block,),
            (own, mate, *marks, after(ahead, *shared[1:]) if shared else ahead, *sent, *earlier),
        )
        if tick == ticks - 2:
            shared = [history[0], *around(history[0])]
    last = [product, *around(product)]
    mine, other = call(
        functools.partial(solve_kernel, chips, tile, ticks),
        (shape(height, ticks * half, WIDE), shape(height, ticks * half, NARROW)),
        (inverse, mate_inverse, *heads, *laters, *came[:-1], after(came[-1], product)),
        [pltpu.VMEM((separator, ticks * half), NARROW)],
    )
    out = shape(height, ticks * PW, WIDE)
    solved = call(join_kernel, out, (mine, swap(other, rows)))

    def add_up(count, blocks, kind, moved=1):
        mine, other = call(
            functools.partial(update_kernel, tile, count, CORES * slots),
            (shape(height, count * half, WIDE), shape(height, count * half, kind)),
            tuple(blocks),
            [pltpu.VMEM((CORES * height, count * half), WIDE)],
            moved,
        )
        return mine, swap(other, rows)

    passed = (
        *add_up(ticks - 1, [after(shared[0], product), *shared[1:]], NARROW),
        *add_up(1, last, WIDE),
    )
    passed = call(join_kernel, out, passed[:-1] + (after(passed[-1], solved),))
    return solved, passed


def solution(mesh):
    placed = (
        P(("chain", "rows"), None),
        P(("chain", "rows"), None),
        P("rows", None),
        P("chain", "rows", None),
        P("chain", "rows", None, None),
        P("chain", "rows"),
        P("chain", None),
        P("chain"),
    )
    return jax.shard_map(
        body,
        mesh=mesh,
        in_specs=placed,
        out_specs=(P(("chain", "rows"), None), P(("chain", "rows"), None)),
        check_vma=False,
    )
```

```python
import functools

import jax
import jax.numpy as jnp
from jax import lax
from jax.experimental import pallas as pl
from jax.experimental.pallas import tpu as pltpu
from jax.sharding import PartitionSpec as P

PW = 256
NOTE = 16
CORES = 2
WIDE = jnp.float32
NARROW = jnp.bfloat16


def partner(chip, offset, chips):
    if chips & (chips - 1) == 0:
        return chip ^ offset
    return (chip + offset) % chips


def multiply(matrix, vector):
    return jnp.dot(matrix, vector, preferred_element_type=WIDE)


def after(value, *others):
    return lax.optimization_barrier((value, *others))[0]


def hop(block, offset_of, step, ends):
    chips, chain = ends
    route = []
    for stage in range(chain - step):
        for chip in range(chips):
            for core in range(CORES):
                goal = partner(chip, offset_of(core), chips)
                source = (stage * chips + chip) * CORES + core
                target = ((stage + step) * chips + goal) * CORES + core
                route.append((source, target))
    return lax.ppermute(block, ("chain", "rows"), route)


def swap(block, rows):
    return lax.ppermute(block, "rows", [(i, i ^ 1) for i in range(rows)])


def place():
    me = lax.axis_index("rows")
    return me, lax.div(me, CORES), lax.rem(me, CORES)


def source_row(offsets, side, chips):
    _, chip, core = place()
    if chips & (chips - 1):
        other = lax.rem(chip + chips - offsets[0], chips)
    else:
        other = chip ^ jnp.where(core == 0, offsets[0], offsets[1])
    return other * CORES + (core if side == 0 else 1 - core)


def straight(chips):
    return [[(offset, offset)] for offset in range(chips)]


def doubling(chips):
    bits = chips.bit_length() - 1
    known, pieces, phases = [(0, 0)], [[(0, 0)]], []
    for phase in range(bits):
        step = (1 << phase, 1 << (phase + 1) % bits)
        phases.append(step)
        pieces.append([(a ^ step[0], b ^ step[1]) for a, b in known])
        known = known + pieces[-1]
    return pieces, phases


def lay_pairs(whole, columns, pieces, origins, chips, start=0):
    height = whole.shape[0] // chips // CORES
    for piece, sources in zip(pieces, origins):
        stride = piece.shape[0] // len(sources)
        for index, offsets in enumerate(sources):
            for side in range(CORES):
                row = source_row(offsets, side, chips)
                rows = pl.ds(pl.multiple_of(row * height, height), height)
                first = index * stride + start + side * height
                whole[rows, columns] = piece[first : first + height]


def is_live(order, count, slot):
    found = jnp.int32(0)
    for k in range(order.shape[1]):
        hit = jnp.logical_and(order[0, k] == slot, k < count[0])
        found = jnp.where(hit, jnp.int32(1), found)
    return found


def mark_kernel(slots, own_target, mate_target, order, count, notes, alive):
    me, _, core = place()
    for side, targets in enumerate((own_target, mate_target)):
        row = me if side == 0 else me + 1 - 2 * core
        for slot in range(slots):
            index = side * slots + slot
            rows = slice(index * NOTE, (index + 1) * NOTE)
            note = jnp.full((NOTE, notes.shape[1]), targets[0, slot], jnp.int32)
            notes[rows] = note.astype(WIDE).astype(NARROW)
            live = is_live(order, count, row * slots + slot)
            alive[index : index + 1] = jnp.full((1, notes.shape[1]), live).astype(WIDE)


def write_tiles(out, products, notes, alive, tile):
    rows = products.shape[0]
    for index in range(rows // tile):
        here = slice(index * tile, (index + 1) * tile)
        kept = jnp.where(alive[index : index + 1] > 0, products[here], 0.0)
        out[here] = kept.astype(NARROW)
    out[rows:] = notes[...]


def read_targets(sent, count):
    first = sent.shape[0] - count * NOTE
    found = []
    for index in range(count):
        note = sent[first + index * NOTE : first + (index + 1) * NOTE, 0:128]
        found.append(note.astype(WIDE).astype(jnp.int32)[0, 0])
    return found


def spread(matrices, sent, tile):
    count = sent[0].shape[0] // (tile + NOTE)
    targets = [t for one in sent for t in read_targets(one, count)]
    picked = [
        jnp.concatenate(
            [m[:, pl.ds(pl.multiple_of(t * tile, tile), tile)] for t in targets], axis=1
        )
        for m in matrices
    ]
    tiles = jnp.concatenate([one[: count * tile] for one in sent], axis=0)
    return multiply(jnp.concatenate(picked, axis=0), tiles)


def pair_kernel(panels, own, mate, out):
    height = own.shape[0] // panels
    for panel in range(panels):
        rows = slice(panel * height, (panel + 1) * height)
        first = panel * CORES * height
        out[first : first + height] = own[rows]
        out[first + height : first + CORES * height] = mate[rows]


def stack_kernel(parts, *refs):
    out, first = refs[-1], 0
    for (start, size), ref in zip(parts, refs[:-1]):
        out[first : first + size] = ref[start : start + size]
        first += size


def first_kernel(chips, tile, *refs):
    own, mate, notes, alive = refs[:4]
    pieces, out, whole = refs[4:-2], refs[-2], refs[-1]
    lay_pairs(whole, slice(0, whole.shape[1]), pieces, straight(chips), chips)
    tiles = jnp.concatenate([own[...], mate[...]], axis=0)
    products = multiply(tiles, whole[...])
    write_tiles(out, products, notes, alive, tile)


def ahead_kernel(chips, origins, starts, *refs):
    own, mate = refs[:2]
    pieces, out, whole = refs[2:-2], refs[-2], refs[-1]
    for piece, sources, start in zip(pieces, origins, starts):
        lay_pairs(whole, slice(0, whole.shape[1]), [piece], [sources], chips, start)
    tiles = jnp.concatenate([own[...], mate[...]], axis=0)
    out[...] = multiply(tiles, whole[...])


def next_kernel(chips, tile, *refs):
    own, mate, notes, alive, ahead = refs[:5]
    sent, rest = refs[5 : 5 + chips], refs[5 + chips :]
    past, outs = rest[: len(rest) // 2], rest[len(rest) // 2 :]
    products = ahead[...]
    products = products - spread((own, mate), sent, tile)
    out = outs[0]
    write_tiles(out, products, notes, alive, tile)
    rows = products.shape[0]
    for index, one in enumerate([*past, out] if past else []):
        outs[1][index * rows : (index + 1) * rows] = one[:rows]
    if past:
        outs[1][(len(past) + 1) * rows :] = notes[...]


def solve_kernel(chips, tile, ticks, origins, starts, *refs):
    inverse, mate = refs[:2]
    heads, (out, other, whole) = refs[2 : 2 + len(origins)], refs[-3:]
    sent = refs[2 + len(origins) : -3]
    half = PW // CORES
    height = out.shape[0]
    for piece, (tick, sources), start in zip(heads, origins, starts):
        columns = slice(tick * half, (tick + 1) * half)
        lay_pairs(whole, columns, [piece], [sources], chips, start)
    matrix = jnp.concatenate([inverse[...], mate[...]], axis=0)
    solved = multiply(matrix, whole[...])
    for tick in range(ticks):
        columns = slice(tick * half, (tick + 1) * half)
        one_tick = solved[:, columns]
        if tick:
            here = sent[(tick - 1) * chips : tick * chips]
            one_tick = one_tick - spread((inverse, mate), here, tile)
        out[:, columns] = one_tick[:height]
        other[:, columns] = one_tick[height:].astype(other.dtype)


def update_kernel(tile, ticks, count, *refs):
    sent, (out, other, total) = refs[:-3], refs[-3:]
    half = PW // CORES
    height = out.shape[0]
    _, chip, core = place()
    size = total.shape[0]
    total[...] = jnp.zeros(total.shape, total.dtype)
    block_rows = count * (ticks * tile + NOTE)
    blocks = [
        one.at[first : first + block_rows]
        for one in sent
        for first in range(0, one.shape[0], block_rows)
    ]
    for one in blocks:
        targets = read_targets(one, count)
        for index in range(ticks * count):
            tick, target = index // count, targets[index % count]
            columns = slice(tick * half, (tick + 1) * half)
            base = index * tile
            if size >= tile:
                held = size // tile
                spot = target - chip * held

                @pl.when(jnp.logical_and(spot >= 0, spot < held))
                def _(one=one, base=base, spot=spot, columns=columns):
                    rows = pl.ds(pl.multiple_of(spot * tile, tile), tile)
                    total[rows, columns] += one[base : base + tile].astype(WIDE)

            else:
                shares = tile // size
                start = base + lax.rem(chip, shares) * size

                @pl.when(target == lax.div(chip, shares))
                def _(one=one, start=start, columns=columns):
                    rows = pl.ds(pl.multiple_of(start, NOTE), size)
                    total[:, columns] += one[rows].astype(WIDE)

    out[...] = total[pl.ds(pl.multiple_of(core * height, height), height)]
    rest = total[pl.ds(pl.multiple_of((1 - core) * height, height), height)]
    other[...] = rest.astype(other.dtype)


def join_kernel(*refs):
    half = PW // CORES
    _, _, core = place()
    out, tick = refs[-1], 0
    for own, mate in zip(refs[0:-1:2], refs[1:-1:2]):
        for index in range(own.shape[1] // half):
            columns = slice(index * half, (index + 1) * half)
            for side, block in ((core, own), (1 - core, mate)):
                start = pl.multiple_of(tick * PW + side * half, half)
                out[:, pl.ds(start, half)] = block[:, columns].astype(out.dtype)
            tick += 1


def call(kernel, out_shape, args, scratch=(), moved=1):
    in_specs = [
        pl.BlockSpec(memory_space=pltpu.SMEM if a.dtype == jnp.int32 else pltpu.VMEM)
        for a in args
    ]
    return pl.pallas_call(
        kernel,
        out_shape=out_shape,
        in_specs=in_specs,
        out_specs=jax.tree.map(lambda _: pl.BlockSpec(memory_space=pltpu.VMEM), out_shape),
        scratch_shapes=list(scratch),
        compiler_params=pltpu.CompilerParams(vmem_limit_bytes=40 * 1024 * 1024),
        cost_estimate=pl.CostEstimate(flops=moved * 1000, bytes_accessed=moved, transcendentals=0),
    )(*args)


def body(
    right_side,
    entering,
    first_updates,
    diag_inverse,
    tile_blocks,
    target_row_blocks,
    tile_usage_order,
    live_tile_count,
):
    rows, chain = lax.axis_size("rows"), lax.axis_size("chain")
    chips = rows // CORES
    slots, tile, separator = tile_blocks.shape[1:]
    height = right_side.shape[0]
    ticks = right_side.shape[1] // PW
    half = PW // CORES
    inverse = diag_inverse[0]
    own = tile_blocks[0].reshape(slots * tile, separator)
    ends = (chips, chain)

    def around(block):
        return [
            hop(block, lambda core, offset=offset: offset, 0, ends) for offset in range(1, chips)
        ]

    def shape(height, width, kind):
        return jax.ShapeDtypeStruct((height, width), kind)

    is_low = lax.rem(lax.axis_index("rows"), CORES) == 0
    is_first = (lax.axis_index("chain") == 0).astype(WIDE)

    def pair_up(panels, *others):
        count = len(panels)
        split = [(one[:, :half], one[:, half:]) for one in panels]
        mine = jnp.concatenate([jnp.where(is_low, a, b) for a, b in split], axis=0)
        other = jnp.concatenate([jnp.where(is_low, b, a) for a, b in split], axis=0)
        return call(
            functools.partial(pair_kernel, count),
            shape(count * CORES * height, half, NARROW),
            (after(mine, *others) if others else mine, swap(other, rows)),
        )

    def panel(tick):
        return right_side[:, tick * PW : (tick + 1) * PW].astype(WIDE)

    head = pair_up([(panel(0) - entering).astype(NARROW)])
    heads = [head, *around(head)]
    mate = swap(own, rows)
    mate_target = swap(target_row_blocks, rows)
    mate_inverse = swap(inverse, rows)
    marks = call(
        functools.partial(mark_kernel, slots),
        (
            shape(CORES * slots * NOTE, half, NARROW),
            shape(CORES * slots, half, WIDE),
        ),
        (target_row_blocks, mate_target, tile_usage_order, live_tile_count),
    )
    rest = [
        (panel(t) - is_first * first_updates[:, (t - 1) * PW : t * PW]).astype(NARROW)
        for t in range(1, ticks)
    ]
    rest = after(pair_up(rest, mate, mate_inverse, marks[1]), *heads[1:])
    pair_rows = CORES * height
    origins, phases = doubling(chips)

    def phase(block, index):
        return hop(block, lambda core: phases[index][core], 0, ends)

    def stacked(parts, args, moved=1):
        rows_in_all = sum(size for _, size in parts)
        kernel = functools.partial(stack_kernel, parts)
        return call(kernel, shape(rows_in_all, half, NARROW), args, (), moved)

    begun = phase(rest, 0)

    def go_on(panel, gate):
        start = panel * pair_rows
        pieces, starts = [rest, begun], [start, start]
        if len(phases) > 1:
            held = stacked([(start, pair_rows)] * 2, (rest, after(begun, gate)))
        for index in range(1, len(phases)):
            pieces.append(phase(held, index))
            starts.append(0)
            if index + 1 < len(phases):
                size = held.shape[0]
                held = stacked([(0, size)] * 2, (held, pieces[-1]))
        return pieces, starts

    def gather(block, gate):
        held, pieces = block, [block]
        for index in range(len(phases)):
            came = phase(held, index)
            pieces.append(came)
            if index + 1 < len(phases):
                size = held.shape[0]
                held = stacked([(0, size)] * 2, (held, after(came, *gate)))
        return pieces

    block_rows = CORES * slots * (tile + NOTE)
    block = shape(block_rows, half, NARROW)
    tile_rows = CORES * slots * tile
    product = call(
        functools.partial(first_kernel, chips, tile),
        block,
        (own, mate, *marks, *heads),
        [pltpu.VMEM((separator, half), NARROW)],
        1,
    )
    came, past, shared, laters = [], [], [], []
    for tick in range(1, ticks):
        past.append(product)
        arrived = hop(product, lambda core: 0, 1, ends)
        sent = [arrived, *around(arrived)]
        came += sent
        if shared:
            shared = gather(shared[0], (arrived,))
        if tick == 1:
            laters.append(go_on(0, arrived))
            laters += [go_on(panel, sent[-1]) for panel in range(1, ticks - 1)]
        pieces, starts = laters[tick - 1]
        ahead = call(
            functools.partial(ahead_kernel, chips, origins, starts),
            shape(tile_rows, half, WIDE),
            (own, mate, *pieces),
            [pltpu.VMEM((separator, half), NARROW)],
        )
        earlier = past if tick == ticks - 2 else []
        history = shape(block_rows + tick * tile_rows, half, NARROW)
        product, *history = call(
            functools.partial(next_kernel, chips, tile),
            (block, history) if earlier else (block,),
            (own, mate, *marks, ahead, *sent, *earlier),
            (),
            1048576 if tick == 1 else 4194304,
        )
        if tick == ticks - 2:
            shared = history
    last = [product, *around(product)]
    columns_of, sources, offsets = list(heads), [(0, one) for one in straight(chips)], [0] * chips
    for tick, (pieces, starts) in enumerate(laters):
        columns_of += pieces
        sources += [(tick + 1, one) for one in origins]
        offsets += starts
    mine, other = call(
        functools.partial(solve_kernel, chips, tile, ticks, sources, offsets),
        (shape(height, ticks * half, WIDE), shape(height, ticks * half, NARROW)),
        (inverse, mate_inverse, *columns_of, *came[:-1], after(came[-1], product)),
        [pltpu.VMEM((separator, ticks * half), NARROW)],
        1,
    )
    out = shape(height, ticks * PW, WIDE)
    solved = call(join_kernel, out, (mine, swap(other, rows)))

    def add_up(count, blocks, kind, moved=1):
        mine, other = call(
            functools.partial(update_kernel, tile, count, CORES * slots),
            (shape(height, count * half, WIDE), shape(height, count * half, kind)),
            tuple(blocks),
            [pltpu.VMEM((CORES * height, count * half), WIDE)],
            moved,
        )
        return mine, swap(other, rows)

    early = add_up(ticks - 1, [after(shared[0], product), *shared[1:]], NARROW)
    passed = (*early, *add_up(1, [after(product, early[0]), *last[1:]], WIDE, 1))
    passed = call(join_kernel, out, passed[:-1] + (after(passed[-1], solved),))
    return solved, passed


def solution(mesh):
    placed = (
        P(("chain", "rows"), None),
        P(("chain", "rows"), None),
        P("rows", None),
        P("chain", "rows", None),
        P("chain", "rows", None, None),
        P("chain", "rows"),
        P("chain", None),
        P("chain"),
    )
    return jax.shard_map(
        body,
        mesh=mesh,
        in_specs=placed,
        out_specs=(P(("chain", "rows"), None), P(("chain", "rows"), None)),
        check_vma=False,
    )
```

```python
import functools

import jax
import jax.numpy as jnp
from jax import lax
from jax.experimental import pallas as pl
from jax.experimental.pallas import tpu as pltpu
from jax.sharding import PartitionSpec as P

PW = 256
NOTE = 16
CORES = 2
WIDE = jnp.float32
NARROW = jnp.bfloat16


def partner(chip, offset, chips):
    if chips & (chips - 1) == 0:
        return chip ^ offset
    return (chip + offset) % chips


def multiply(matrix, vector):
    return jnp.dot(matrix, vector, preferred_element_type=WIDE)


def after(value, *others):
    return lax.optimization_barrier((value, *others))[0]


def hop(block, offset_of, step, ends):
    chips, chain = ends
    route = []
    for stage in range(chain - step):
        for chip in range(chips):
            for core in range(CORES):
                goal = partner(chip, offset_of(core), chips)
                source = (stage * chips + chip) * CORES + core
                target = ((stage + step) * chips + goal) * CORES + core
                route.append((source, target))
    return lax.ppermute(block, ("chain", "rows"), route)


def swap(block, rows):
    return lax.ppermute(block, "rows", [(i, i ^ 1) for i in range(rows)])


def place():
    me = lax.axis_index("rows")
    return me, lax.div(me, CORES), lax.rem(me, CORES)


def source_row(offsets, side, chips):
    _, chip, core = place()
    if chips & (chips - 1):
        other = lax.rem(chip + chips - offsets[0], chips)
    else:
        other = chip ^ jnp.where(core == 0, offsets[0], offsets[1])
    return other * CORES + (core if side == 0 else 1 - core)


def straight(chips):
    return [[(offset, offset)] for offset in range(chips)]


def doubling(chips):
    bits = chips.bit_length() - 1
    known, pieces, phases = [(0, 0)], [[(0, 0)]], []
    for phase in range(bits):
        step = (1 << phase, 1 << (phase + 1) % bits)
        phases.append(step)
        pieces.append([(a ^ step[0], b ^ step[1]) for a, b in known])
        known = known + pieces[-1]
    return pieces, phases


def lay_pairs(whole, columns, pieces, origins, chips, start=0):
    height = whole.shape[0] // chips // CORES
    for piece, sources in zip(pieces, origins):
        stride = piece.shape[0] // len(sources)
        for index, offsets in enumerate(sources):
            for side in range(CORES):
                row = source_row(offsets, side, chips)
                rows = pl.ds(pl.multiple_of(row * height, height), height)
                first = index * stride + start + side * height
                whole[rows, columns] = piece[first : first + height]


def is_live(order, count, slot):
    found = jnp.int32(0)
    for k in range(order.shape[1]):
        hit = jnp.logical_and(order[0, k] == slot, k < count[0])
        found = jnp.where(hit, jnp.int32(1), found)
    return found


def mark_kernel(slots, own_target, mate_target, order, count, notes, alive):
    me, _, core = place()
    for side, targets in enumerate((own_target, mate_target)):
        row = me if side == 0 else me + 1 - 2 * core
        for slot in range(slots):
            index = side * slots + slot
            rows = slice(index * NOTE, (index + 1) * NOTE)
            note = jnp.full((NOTE, notes.shape[1]), targets[0, slot], jnp.int32)
            notes[rows] = note.astype(WIDE).astype(NARROW)
            live = is_live(order, count, row * slots + slot)
            alive[index : index + 1] = jnp.full((1, notes.shape[1]), live).astype(WIDE)


def write_tiles(out, products, notes, alive, tile):
    rows = products.shape[0]
    for index in range(rows // tile):
        here = slice(index * tile, (index + 1) * tile)
        kept = jnp.where(alive[index : index + 1] > 0, products[here], 0.0)
        out[here] = kept.astype(NARROW)
    out[rows:] = notes[...]


def read_targets(sent, count):
    first = sent.shape[0] - count * NOTE
    found = []
    for index in range(count):
        note = sent[first + index * NOTE : first + (index + 1) * NOTE, 0:128]
        found.append(note.astype(WIDE).astype(jnp.int32)[0, 0])
    return found


def spread(matrices, sent, tile):
    count = sent[0].shape[0] // (tile + NOTE)
    targets = [t for one in sent for t in read_targets(one, count)]
    picked = [
        jnp.concatenate(
            [m[:, pl.ds(pl.multiple_of(t * tile, tile), tile)] for t in targets], axis=1
        )
        for m in matrices
    ]
    tiles = jnp.concatenate([one[: count * tile] for one in sent], axis=0)
    return multiply(jnp.concatenate(picked, axis=0), tiles)


def pair_kernel(panels, own, mate, out):
    height = own.shape[0] // panels
    for panel in range(panels):
        rows = slice(panel * height, (panel + 1) * height)
        first = panel * CORES * height
        out[first : first + height] = own[rows]
        out[first + height : first + CORES * height] = mate[rows]


def stack_kernel(parts, *refs):
    out, first = refs[-1], 0
    for (start, size), ref in zip(parts, refs[:-1]):
        out[first : first + size] = ref[start : start + size]
        first += size


def first_kernel(chips, tile, *refs):
    own, mate, notes, alive = refs[:4]
    pieces, out, whole = refs[4:-2], refs[-2], refs[-1]
    lay_pairs(whole, slice(0, whole.shape[1]), pieces, straight(chips), chips)
    tiles = jnp.concatenate([own[...], mate[...]], axis=0)
    products = multiply(tiles, whole[...])
    write_tiles(out, products, notes, alive, tile)


def ahead_kernel(chips, origins, starts, *refs):
    own, mate = refs[:2]
    pieces, out, whole = refs[2:-2], refs[-2], refs[-1]
    for piece, sources, start in zip(pieces, origins, starts):
        lay_pairs(whole, slice(0, whole.shape[1]), [piece], [sources], chips, start)
    tiles = jnp.concatenate([own[...], mate[...]], axis=0)
    out[...] = multiply(tiles, whole[...])


def next_kernel(chips, tile, *refs):
    own, mate, notes, alive, ahead = refs[:5]
    sent, rest = refs[5 : 5 + chips], refs[5 + chips :]
    past, outs = rest[: len(rest) // 2], rest[len(rest) // 2 :]
    products = ahead[...]
    products = products - spread((own, mate), sent, tile)
    out = outs[0]
    write_tiles(out, products, notes, alive, tile)
    rows = products.shape[0]
    for index, one in enumerate([*past, out] if past else []):
        outs[1][index * rows : (index + 1) * rows] = one[:rows]
    if past:
        outs[1][(len(past) + 1) * rows :] = notes[...]


def solve_kernel(chips, tile, ticks, origins, starts, *refs):
    inverse, mate = refs[:2]
    heads, (out, other, whole) = refs[2 : 2 + len(origins)], refs[-3:]
    sent = refs[2 + len(origins) : -3]
    half = PW // CORES
    height = out.shape[0]
    for piece, (tick, sources), start in zip(heads, origins, starts):
        columns = slice(tick * half, (tick + 1) * half)
        lay_pairs(whole, columns, [piece], [sources], chips, start)
    matrix = jnp.concatenate([inverse[...], mate[...]], axis=0)
    solved = multiply(matrix, whole[...])
    for tick in range(ticks):
        columns = slice(tick * half, (tick + 1) * half)
        one_tick = solved[:, columns]
        if tick:
            here = sent[(tick - 1) * chips : tick * chips]
            one_tick = one_tick - spread((inverse, mate), here, tile)
        out[:, columns] = one_tick[:height]
        other[:, columns] = one_tick[height:].astype(other.dtype)


def update_kernel(tile, ticks, count, *refs):
    sent, (out, other, total) = refs[:-3], refs[-3:]
    half = PW // CORES
    height = out.shape[0]
    _, chip, core = place()
    size = total.shape[0]
    total[...] = jnp.zeros(total.shape, total.dtype)
    block_rows = count * (ticks * tile + NOTE)
    blocks = [
        one.at[first : first + block_rows]
        for one in sent
        for first in range(0, one.shape[0], block_rows)
    ]
    for one in blocks:
        targets = read_targets(one, count)
        for index in range(ticks * count):
            tick, target = index // count, targets[index % count]
            columns = slice(tick * half, (tick + 1) * half)
            base = index * tile
            if size >= tile:
                held = size // tile
                spot = target - chip * held

                @pl.when(jnp.logical_and(spot >= 0, spot < held))
                def _(one=one, base=base, spot=spot, columns=columns):
                    rows = pl.ds(pl.multiple_of(spot * tile, tile), tile)
                    total[rows, columns] += one[base : base + tile].astype(WIDE)

            else:
                shares = tile // size
                start = base + lax.rem(chip, shares) * size

                @pl.when(target == lax.div(chip, shares))
                def _(one=one, start=start, columns=columns):
                    rows = pl.ds(pl.multiple_of(start, NOTE), size)
                    total[:, columns] += one[rows].astype(WIDE)

    out[...] = total[pl.ds(pl.multiple_of(core * height, height), height)]
    rest = total[pl.ds(pl.multiple_of((1 - core) * height, height), height)]
    other[...] = rest.astype(other.dtype)


def join_kernel(*refs):
    half = PW // CORES
    _, _, core = place()
    out, tick = refs[-1], 0
    for own, mate in zip(refs[0:-1:2], refs[1:-1:2]):
        for index in range(own.shape[1] // half):
            columns = slice(index * half, (index + 1) * half)
            for side, block in ((core, own), (1 - core, mate)):
                start = pl.multiple_of(tick * PW + side * half, half)
                out[:, pl.ds(start, half)] = block[:, columns].astype(out.dtype)
            tick += 1


def call(kernel, out_shape, args, scratch=(), moved=1):
    in_specs = [
        pl.BlockSpec(memory_space=pltpu.SMEM if a.dtype == jnp.int32 else pltpu.VMEM)
        for a in args
    ]
    return pl.pallas_call(
        kernel,
        out_shape=out_shape,
        in_specs=in_specs,
        out_specs=jax.tree.map(lambda _: pl.BlockSpec(memory_space=pltpu.VMEM), out_shape),
        scratch_shapes=list(scratch),
        compiler_params=pltpu.CompilerParams(vmem_limit_bytes=40 * 1024 * 1024),
        cost_estimate=pl.CostEstimate(flops=moved * 1000, bytes_accessed=moved, transcendentals=0),
    )(*args)


def body(
    right_side,
    entering,
    first_updates,
    diag_inverse,
    tile_blocks,
    target_row_blocks,
    tile_usage_order,
    live_tile_count,
):
    rows, chain = lax.axis_size("rows"), lax.axis_size("chain")
    chips = rows // CORES
    slots, tile, separator = tile_blocks.shape[1:]
    height = right_side.shape[0]
    ticks = right_side.shape[1] // PW
    half = PW // CORES
    inverse = diag_inverse[0]
    own = tile_blocks[0].reshape(slots * tile, separator)
    ends = (chips, chain)

    def around(block):
        return [
            hop(block, lambda core, offset=offset: offset, 0, ends) for offset in range(1, chips)
        ]

    def shape(height, width, kind):
        return jax.ShapeDtypeStruct((height, width), kind)

    is_low = lax.rem(lax.axis_index("rows"), CORES) == 0
    is_first = (lax.axis_index("chain") == 0).astype(WIDE)

    def pair_up(panels, *others):
        count = len(panels)
        split = [(one[:, :half], one[:, half:]) for one in panels]
        mine = jnp.concatenate([jnp.where(is_low, a, b) for a, b in split], axis=0)
        other = jnp.concatenate([jnp.where(is_low, b, a) for a, b in split], axis=0)
        return call(
            functools.partial(pair_kernel, count),
            shape(count * CORES * height, half, NARROW),
            (after(mine, *others) if others else mine, swap(other, rows)),
        )

    def panel(tick):
        return right_side[:, tick * PW : (tick + 1) * PW].astype(WIDE)

    head = pair_up([(panel(0) - entering).astype(NARROW)])
    heads = [head, *around(head)]
    mate = swap(own, rows)
    mate_target = swap(target_row_blocks, rows)
    mate_inverse = swap(inverse, rows)
    marks = call(
        functools.partial(mark_kernel, slots),
        (
            shape(CORES * slots * NOTE, half, NARROW),
            shape(CORES * slots, half, WIDE),
        ),
        (target_row_blocks, mate_target, tile_usage_order, live_tile_count),
        (),
        1,
    )
    rest = [
        (panel(t) - is_first * first_updates[:, (t - 1) * PW : t * PW]).astype(NARROW)
        for t in range(1, ticks)
    ]
    rest = after(pair_up(rest, mate, mate_inverse, marks[1]), *heads[3:])
    pair_rows = CORES * height
    origins, phases = doubling(chips)

    def phase(block, index):
        return hop(block, lambda core: phases[index][core], 0, ends)

    def stacked(parts, args, moved=1):
        rows_in_all = sum(size for _, size in parts)
        kernel = functools.partial(stack_kernel, parts)
        return call(kernel, shape(rows_in_all, half, NARROW), args, (), moved)

    begun = phase(rest, 0)

    def go_on(panel, gate):
        start = panel * pair_rows
        pieces, starts = [rest, begun], [start, start]
        if len(phases) > 1:
            held = stacked([(start, pair_rows)] * 2, (rest, after(begun, gate)))
        for index in range(1, len(phases)):
            pieces.append(phase(held, index))
            starts.append(0)
            if index + 1 < len(phases):
                size = held.shape[0]
                held = stacked([(0, size)] * 2, (held, pieces[-1]))
        return pieces, starts

    def gather(block, gate):
        held, pieces = block, [block]
        for index in range(len(phases)):
            came = phase(held, index)
            pieces.append(came)
            if index + 1 < len(phases):
                size = held.shape[0]
                held = stacked([(0, size)] * 2, (held, after(came, *gate)))
        return pieces

    block_rows = CORES * slots * (tile + NOTE)
    block = shape(block_rows, half, NARROW)
    tile_rows = CORES * slots * tile
    product = call(
        functools.partial(first_kernel, chips, tile),
        block,
        (own, mate, *marks, *heads),
        [pltpu.VMEM((separator, half), NARROW)],
        8388608,
    )
    came, past, shared, laters = [], [], [], []
    for tick in range(1, ticks):
        past.append(product)
        arrived = hop(product, lambda core: 0, 1, ends)
        if tick == 1:
            arrived = stacked([(0, block_rows)], (arrived,), 8388608)
        sent = [arrived, *around(arrived)]
        came += sent
        if shared:
            shared = gather(shared[0], (arrived,))
        if tick == 1:
            laters.append(go_on(0, product))
            laters += [go_on(panel, sent[-1]) for panel in range(1, ticks - 1)]
        pieces, starts = laters[tick - 1]
        ahead = call(
            functools.partial(ahead_kernel, chips, origins, starts),
            shape(tile_rows, half, WIDE),
            (own, mate, *pieces),
            [pltpu.VMEM((separator, half), NARROW)],
        )
        earlier = past if tick == ticks - 2 else []
        history = shape(block_rows + tick * tile_rows, half, NARROW)
        product, *history = call(
            functools.partial(next_kernel, chips, tile),
            (block, history) if earlier else (block,),
            (own, mate, *marks, ahead, *sent, *earlier),
            (),
            1048576 if tick == 1 else 4194304,
        )
        if tick == ticks - 2:
            shared = history
    last = [product, *around(product)]
    columns_of, sources, offsets = list(heads), [(0, one) for one in straight(chips)], [0] * chips
    for tick, (pieces, starts) in enumerate(laters):
        columns_of += pieces
        sources += [(tick + 1, one) for one in origins]
        offsets += starts
    mine, other = call(
        functools.partial(solve_kernel, chips, tile, ticks, sources, offsets),
        (shape(height, ticks * half, WIDE), shape(height, ticks * half, NARROW)),
        (inverse, mate_inverse, *columns_of, *came[:-1], after(came[-1], product)),
        [pltpu.VMEM((separator, ticks * half), NARROW)],
        1,
    )
    out = shape(height, ticks * PW, WIDE)
    solved = call(join_kernel, out, (mine, swap(other, rows)))

    def add_up(count, blocks, kind, moved=1):
        mine, other = call(
            functools.partial(update_kernel, tile, count, CORES * slots),
            (shape(height, count * half, WIDE), shape(height, count * half, kind)),
            tuple(blocks),
            [pltpu.VMEM((CORES * height, count * half), WIDE)],
            moved,
        )
        return mine, swap(other, rows)

    early = add_up(ticks - 1, [after(shared[0], product), *shared[1:]], NARROW)
    passed = (*early, *add_up(1, [after(product, early[0]), *last[1:]], WIDE, 1))
    passed = call(join_kernel, out, passed[:-1] + (after(passed[-1], solved),))
    return solved, passed


def solution(mesh):
    placed = (
        P(("chain", "rows"), None),
        P(("chain", "rows"), None),
        P("rows", None),
        P("chain", "rows", None),
        P("chain", "rows", None, None),
        P("chain", "rows"),
        P("chain", None),
        P("chain"),
    )
    return jax.shard_map(
        body,
        mesh=mesh,
        in_specs=placed,
        out_specs=(P(("chain", "rows"), None), P(("chain", "rows"), None)),
        check_vma=False,
    )
```

```python
import functools

import jax
import jax.numpy as jnp
from jax import lax
from jax.experimental import pallas as pl
from jax.experimental.pallas import tpu as pltpu
from jax.sharding import PartitionSpec as P

PW = 256
NOTE = 16
CORES = 2
WIDE = jnp.float32
NARROW = jnp.bfloat16
LITTLE, SOME, LONG = 1 << 20, 4 << 20, 8 << 20


def partner(chip, offset, chips):
    if chips & (chips - 1) == 0:
        return chip ^ offset
    return (chip + offset) % chips


def multiply(matrix, vector):
    return jnp.dot(matrix, vector, preferred_element_type=WIDE)


def after(value, *others):
    return lax.optimization_barrier((value, *others))[0]


def hop(block, offset_of, step, ends):
    chips, chain = ends
    route = []
    for stage in range(chain - step):
        for chip in range(chips):
            for core in range(CORES):
                goal = partner(chip, offset_of(core), chips)
                source = (stage * chips + chip) * CORES + core
                target = ((stage + step) * chips + goal) * CORES + core
                route.append((source, target))
    return lax.ppermute(block, ("chain", "rows"), route)


def swap(block, rows):
    return lax.ppermute(block, "rows", [(i, i ^ 1) for i in range(rows)])


def place():
    me = lax.axis_index("rows")
    return me, lax.div(me, CORES), lax.rem(me, CORES)


def source_row(offsets, side, chips):
    _, chip, core = place()
    if chips & (chips - 1):
        other = lax.rem(chip + chips - offsets[0], chips)
    else:
        other = chip ^ jnp.where(core == 0, offsets[0], offsets[1])
    return other * CORES + (core if side == 0 else 1 - core)


def straight(chips):
    return [[(offset, offset)] for offset in range(chips)]


def doubling(chips):
    bits = chips.bit_length() - 1
    known, pieces, phases = [(0, 0)], [[(0, 0)]], []
    for phase in range(bits):
        step = (1 << phase, 1 << (phase + 1) % bits)
        phases.append(step)
        pieces.append([(a ^ step[0], b ^ step[1]) for a, b in known])
        known = known + pieces[-1]
    return pieces, phases


def lay_pairs(whole, columns, pieces, origins, chips, start=0):
    height = whole.shape[0] // chips // CORES
    for piece, sources in zip(pieces, origins):
        stride = piece.shape[0] // len(sources)
        for index, offsets in enumerate(sources):
            for side in range(CORES):
                row = source_row(offsets, side, chips)
                rows = pl.ds(pl.multiple_of(row * height, height), height)
                first = index * stride + start + side * height
                whole[rows, columns] = piece[first : first + height]


def is_live(order, count, slot):
    found = jnp.int32(0)
    for k in range(order.shape[1]):
        hit = jnp.logical_and(order[0, k] == slot, k < count[0])
        found = jnp.where(hit, jnp.int32(1), found)
    return found


def mark_kernel(slots, own_target, mate_target, order, count, notes, alive):
    me, _, core = place()
    for side, targets in enumerate((own_target, mate_target)):
        row = me if side == 0 else me + 1 - 2 * core
        for slot in range(slots):
            index = side * slots + slot
            rows = slice(index * NOTE, (index + 1) * NOTE)
            note = jnp.full((NOTE, notes.shape[1]), targets[0, slot], jnp.int32)
            notes[rows] = note.astype(WIDE).astype(NARROW)
            live = is_live(order, count, row * slots + slot)
            alive[index : index + 1] = jnp.full((1, notes.shape[1]), live).astype(WIDE)


def write_tiles(out, products, notes, alive, tile):
    rows = products.shape[0]
    for index in range(rows // tile):
        here = slice(index * tile, (index + 1) * tile)
        kept = jnp.where(alive[index : index + 1] > 0, products[here], 0.0)
        out[here] = kept.astype(NARROW)
    out[rows:] = notes[...]


def read_targets(sent, count):
    first = sent.shape[0] - count * NOTE
    found = []
    for index in range(count):
        note = sent[first + index * NOTE : first + (index + 1) * NOTE, 0:128]
        found.append(note.astype(WIDE).astype(jnp.int32)[0, 0])
    return found


def spread(matrices, sent, tile):
    count = sent[0].shape[0] // (tile + NOTE)
    targets = [t for one in sent for t in read_targets(one, count)]
    picked = [
        jnp.concatenate(
            [m[:, pl.ds(pl.multiple_of(t * tile, tile), tile)] for t in targets], axis=1
        )
        for m in matrices
    ]
    tiles = jnp.concatenate([one[: count * tile] for one in sent], axis=0)
    return multiply(jnp.concatenate(picked, axis=0), tiles)


def pair_kernel(panels, own, mate, out):
    height = own.shape[0] // panels
    for panel in range(panels):
        rows = slice(panel * height, (panel + 1) * height)
        first = panel * CORES * height
        out[first : first + height] = own[rows]
        out[first + height : first + CORES * height] = mate[rows]


def stack_kernel(parts, *refs):
    out, first = refs[-1], 0
    for (start, size), ref in zip(parts, refs[:-1]):
        out[first : first + size] = ref[start : start + size]
        first += size


def lay_kernel(chips, *refs):
    lay_pairs(refs[-1], slice(0, refs[-1].shape[1]), refs[:-1], straight(chips), chips)


def first_kernel(tile, own, mate, notes, alive, whole, out):
    tiles = jnp.concatenate([own[...], mate[...]], axis=0)
    write_tiles(out, multiply(tiles, whole[...]), notes, alive, tile)


def ahead_kernel(chips, origins, starts, *refs):
    own, mate = refs[:2]
    pieces, out, whole = refs[2:-2], refs[-2], refs[-1]
    for piece, sources, start in zip(pieces, origins, starts):
        lay_pairs(whole, slice(0, whole.shape[1]), [piece], [sources], chips, start)
    tiles = jnp.concatenate([own[...], mate[...]], axis=0)
    out[...] = multiply(tiles, whole[...])


def next_kernel(chips, tile, *refs):
    own, mate, notes, alive, ahead = refs[:5]
    sent, rest = refs[5 : 5 + chips], refs[5 + chips :]
    past, outs = rest[: len(rest) // 2], rest[len(rest) // 2 :]
    products = ahead[...]
    products = products - spread((own, mate), sent, tile)
    out = outs[0]
    write_tiles(out, products, notes, alive, tile)
    rows = products.shape[0]
    for index, one in enumerate([*past, out] if past else []):
        outs[1][index * rows : (index + 1) * rows] = one[:rows]
    if past:
        outs[1][(len(past) + 1) * rows :] = notes[...]


def solve_kernel(chips, tile, ticks, origins, starts, *refs):
    inverse, mate = refs[:2]
    heads, (out, other, whole) = refs[2 : 2 + len(origins)], refs[-3:]
    sent = refs[2 + len(origins) : -3]
    half = PW // CORES
    height = out.shape[0]
    for piece, (tick, sources), start in zip(heads, origins, starts):
        columns = slice(tick * half, (tick + 1) * half)
        lay_pairs(whole, columns, [piece], [sources], chips, start)
    matrix = jnp.concatenate([inverse[...], mate[...]], axis=0)
    solved = multiply(matrix, whole[...])
    for tick in range(ticks):
        columns = slice(tick * half, (tick + 1) * half)
        one_tick = solved[:, columns]
        if tick:
            here = sent[(tick - 1) * chips : tick * chips]
            one_tick = one_tick - spread((inverse, mate), here, tile)
        out[:, columns] = one_tick[:height]
        other[:, columns] = one_tick[height:].astype(other.dtype)


def update_kernel(tile, ticks, count, *refs):
    sent, (out, other, total) = refs[:-3], refs[-3:]
    half = PW // CORES
    height = out.shape[0]
    _, chip, core = place()
    size = total.shape[0]
    total[...] = jnp.zeros(total.shape, total.dtype)
    block_rows = count * (ticks * tile + NOTE)
    blocks = [
        one.at[first : first + block_rows]
        for one in sent
        for first in range(0, one.shape[0], block_rows)
    ]
    for one in blocks:
        targets = read_targets(one, count)
        for index in range(ticks * count):
            tick, target = index // count, targets[index % count]
            columns = slice(tick * half, (tick + 1) * half)
            base = index * tile
            if size >= tile:
                held = size // tile
                spot = target - chip * held

                @pl.when(jnp.logical_and(spot >= 0, spot < held))
                def _(one=one, base=base, spot=spot, columns=columns):
                    rows = pl.ds(pl.multiple_of(spot * tile, tile), tile)
                    total[rows, columns] += one[base : base + tile].astype(WIDE)

            else:
                shares = tile // size
                start = base + lax.rem(chip, shares) * size

                @pl.when(target == lax.div(chip, shares))
                def _(one=one, start=start, columns=columns):
                    rows = pl.ds(pl.multiple_of(start, NOTE), size)
                    total[:, columns] += one[rows].astype(WIDE)

    out[...] = total[pl.ds(pl.multiple_of(core * height, height), height)]
    rest = total[pl.ds(pl.multiple_of((1 - core) * height, height), height)]
    other[...] = rest.astype(other.dtype)


def join_kernel(*refs):
    half = PW // CORES
    _, _, core = place()
    out, tick = refs[-1], 0
    for own, mate in zip(refs[0:-1:2], refs[1:-1:2]):
        for index in range(own.shape[1] // half):
            columns = slice(index * half, (index + 1) * half)
            for side, block in ((core, own), (1 - core, mate)):
                start = pl.multiple_of(tick * PW + side * half, half)
                out[:, pl.ds(start, half)] = block[:, columns].astype(out.dtype)
            tick += 1


def call(kernel, out_shape, args, scratch=(), weight=1):
    in_specs = [
        pl.BlockSpec(memory_space=pltpu.SMEM if a.dtype == jnp.int32 else pltpu.VMEM)
        for a in args
    ]
    return pl.pallas_call(
        kernel,
        out_shape=out_shape,
        in_specs=in_specs,
        out_specs=jax.tree.map(lambda _: pl.BlockSpec(memory_space=pltpu.VMEM), out_shape),
        scratch_shapes=list(scratch),
        compiler_params=pltpu.CompilerParams(vmem_limit_bytes=40 * 1024 * 1024),
        cost_estimate=pl.CostEstimate(flops=weight * 1000, bytes_accessed=weight, transcendentals=0),
    )(*args)


def body(
    right_side,
    entering,
    first_updates,
    diag_inverse,
    tile_blocks,
    target_row_blocks,
    tile_usage_order,
    live_tile_count,
):
    rows, chain = lax.axis_size("rows"), lax.axis_size("chain")
    chips = rows // CORES
    slots, tile, separator = tile_blocks.shape[1:]
    height = right_side.shape[0]
    ticks = right_side.shape[1] // PW
    half = PW // CORES
    inverse = diag_inverse[0]
    own = tile_blocks[0].reshape(slots * tile, separator)
    ends = (chips, chain)

    def around(block):
        return [
            hop(block, lambda core, offset=offset: offset, 0, ends) for offset in range(1, chips)
        ]

    def shape(height, width, kind):
        return jax.ShapeDtypeStruct((height, width), kind)

    is_low = lax.rem(lax.axis_index("rows"), CORES) == 0
    is_first = (lax.axis_index("chain") == 0).astype(WIDE)

    def pair_up(panels, *others):
        count = len(panels)
        split = [(one[:, :half], one[:, half:]) for one in panels]
        mine = jnp.concatenate([jnp.where(is_low, a, b) for a, b in split], axis=0)
        other = jnp.concatenate([jnp.where(is_low, b, a) for a, b in split], axis=0)
        return call(
            functools.partial(pair_kernel, count),
            shape(count * CORES * height, half, NARROW),
            (after(mine, *others) if others else mine, swap(other, rows)),
        )

    def panel(tick):
        return right_side[:, tick * PW : (tick + 1) * PW].astype(WIDE)

    head = pair_up([(panel(0) - entering).astype(NARROW)])
    heads = [head, *around(head)]
    mate = swap(own, rows)
    mate_target = swap(target_row_blocks, rows)
    mate_inverse = swap(inverse, rows)
    marks = call(
        functools.partial(mark_kernel, slots),
        (
            shape(CORES * slots * NOTE, half, NARROW),
            shape(CORES * slots, half, WIDE),
        ),
        (target_row_blocks, mate_target, tile_usage_order, live_tile_count),
    )
    rest = [
        (panel(t) - is_first * first_updates[:, (t - 1) * PW : t * PW]).astype(NARROW)
        for t in range(1, ticks)
    ]
    rest = after(pair_up(rest, marks[1]), *heads[3:])
    pair_rows = CORES * height
    origins, phases = doubling(chips)

    def phase(block, index):
        return hop(block, lambda core: phases[index][core], 0, ends)

    def stacked(parts, args, weight=1):
        rows_in_all = sum(size for _, size in parts)
        kernel = functools.partial(stack_kernel, parts)
        return call(kernel, shape(rows_in_all, half, NARROW), args, (), weight)

    begun = phase(rest, 0)

    def go_on(panel, gate):
        start = panel * pair_rows
        pieces, starts = [rest, begun], [start, start]
        if len(phases) > 1:
            held = stacked([(start, pair_rows)] * 2, (rest, after(begun, gate)))
        for index in range(1, len(phases)):
            pieces.append(phase(held, index))
            starts.append(0)
            if index + 1 < len(phases):
                size = held.shape[0]
                held = stacked([(0, size)] * 2, (held, pieces[-1]))
        return pieces, starts

    def gather(block, gate):
        held, pieces = block, [block]
        for index in range(len(phases)):
            came = phase(held, index)
            pieces.append(came)
            if index + 1 < len(phases):
                size = held.shape[0]
                held = stacked([(0, size)] * 2, (held, after(came, *gate)))
        return pieces

    block_rows = CORES * slots * (tile + NOTE)
    block = shape(block_rows, half, NARROW)
    tile_rows = CORES * slots * tile
    whole = call(
        functools.partial(lay_kernel, chips),
        shape(separator, half, NARROW),
        tuple(heads),
        (),
        LONG,
    )
    product = call(
        functools.partial(first_kernel, tile),
        block,
        (after(own, mate_inverse), mate, *marks, whole),
        (),
        LONG,
    )
    came, past, shared, laters = [], [], [], []
    for tick in range(1, ticks):
        past.append(product)
        arrived = hop(product, lambda core: 0, 1, ends)
        if tick == 1:
            arrived = stacked([(0, block_rows)], (arrived,), LONG)
        sent = [arrived, *around(arrived)]
        came += sent
        if shared:
            shared = gather(shared[0], (arrived,))
        if tick == 1:
            laters.append(go_on(0, product))
            laters += [go_on(panel, sent[-1]) for panel in range(1, ticks - 1)]
        pieces, starts = laters[tick - 1]
        ahead = call(
            functools.partial(ahead_kernel, chips, origins, starts),
            shape(tile_rows, half, WIDE),
            (own, mate, *pieces),
            [pltpu.VMEM((separator, half), NARROW)],
        )
        earlier = past if tick == ticks - 2 else []
        history = shape(block_rows + tick * tile_rows, half, NARROW)
        product, *history = call(
            functools.partial(next_kernel, chips, tile),
            (block, history) if earlier else (block,),
            (own, mate, *marks, ahead, *sent, *earlier),
            (),
            LITTLE if tick == 1 else SOME,
        )
        if tick == ticks - 2:
            shared = history
    last = [product, *around(product)]
    columns_of, sources, offsets = list(heads), [(0, one) for one in straight(chips)], [0] * chips
    for tick, (pieces, starts) in enumerate(laters):
        columns_of += pieces
        sources += [(tick + 1, one) for one in origins]
        offsets += starts
    mine, other = call(
        functools.partial(solve_kernel, chips, tile, ticks, sources, offsets),
        (shape(height, ticks * half, WIDE), shape(height, ticks * half, NARROW)),
        (inverse, mate_inverse, *columns_of, *came[:-1], after(came[-1], product)),
        [pltpu.VMEM((separator, ticks * half), NARROW)],
    )
    out = shape(height, ticks * PW, WIDE)
    solved = call(join_kernel, out, (mine, swap(other, rows)))

    def add_up(count, blocks, kind):
        mine, other = call(
            functools.partial(update_kernel, tile, count, CORES * slots),
            (shape(height, count * half, WIDE), shape(height, count * half, kind)),
            tuple(blocks),
            [pltpu.VMEM((CORES * height, count * half), WIDE)],
        )
        return mine, swap(other, rows)

    early = add_up(ticks - 1, [after(shared[0], product), *shared[1:]], NARROW)
    passed = (*early, *add_up(1, [after(product, early[0]), *last[1:]], WIDE))
    passed = call(join_kernel, out, passed[:-1] + (after(passed[-1], solved),))
    return solved, passed


def solution(mesh):
    placed = (
        P(("chain", "rows"), None),
        P(("chain", "rows"), None),
        P("rows", None),
        P("chain", "rows", None),
        P("chain", "rows", None, None),
        P("chain", "rows"),
        P("chain", None),
        P("chain"),
    )
    return jax.shard_map(
        body,
        mesh=mesh,
        in_specs=placed,
        out_specs=(P(("chain", "rows"), None), P(("chain", "rows"), None)),
        check_vma=False,
    )
```

```python
import functools

import jax
import jax.numpy as jnp
from jax import lax
from jax.experimental import pallas as pl
from jax.experimental.pallas import tpu as pltpu
from jax.sharding import PartitionSpec as P

PW = 256
NOTE = 16
CORES = 2
WIDE = jnp.float32
NARROW = jnp.bfloat16
LITTLE, SOME, LONG = 1 << 20, 4 << 20, 8 << 20


def partner(chip, offset, chips):
    if chips & (chips - 1) == 0:
        return chip ^ offset
    return (chip + offset) % chips


def multiply(matrix, vector):
    return jnp.dot(matrix, vector, preferred_element_type=WIDE)


def after(value, *others):
    return lax.optimization_barrier((value, *others))[0]


def hop(block, offset_of, step, ends):
    chips, chain = ends
    route = []
    for stage in range(chain - step):
        for chip in range(chips):
            for core in range(CORES):
                goal = partner(chip, offset_of(core), chips)
                source = (stage * chips + chip) * CORES + core
                target = ((stage + step) * chips + goal) * CORES + core
                route.append((source, target))
    return lax.ppermute(block, ("chain", "rows"), route)


def swap(block, rows):
    return lax.ppermute(block, "rows", [(i, i ^ 1) for i in range(rows)])


def place():
    me = lax.axis_index("rows")
    return me, lax.div(me, CORES), lax.rem(me, CORES)


def source_row(offsets, side, chips):
    _, chip, core = place()
    if chips & (chips - 1):
        other = lax.rem(chip + chips - offsets[0], chips)
    else:
        other = chip ^ jnp.where(core == 0, offsets[0], offsets[1])
    return other * CORES + (core if side == 0 else 1 - core)


def straight(chips):
    return [[(offset, offset)] for offset in range(chips)]


def doubling(chips):
    bits = chips.bit_length() - 1
    known, pieces, phases = [(0, 0)], [[(0, 0)]], []
    for phase in range(bits):
        step = (1 << phase, 1 << (phase + 1) % bits)
        phases.append(step)
        pieces.append([(a ^ step[0], b ^ step[1]) for a, b in known])
        known = known + pieces[-1]
    return pieces, phases


def lay_pairs(whole, columns, pieces, origins, chips, start=0):
    height = whole.shape[0] // chips // CORES
    for piece, sources in zip(pieces, origins):
        stride = piece.shape[0] // len(sources)
        for index, offsets in enumerate(sources):
            for side in range(CORES):
                row = source_row(offsets, side, chips)
                rows = pl.ds(pl.multiple_of(row * height, height), height)
                first = index * stride + start + side * height
                whole[rows, columns] = piece[first : first + height]


def is_live(order, count, slot):
    found = jnp.int32(0)
    for k in range(order.shape[1]):
        hit = jnp.logical_and(order[0, k] == slot, k < count[0])
        found = jnp.where(hit, jnp.int32(1), found)
    return found


def mark_kernel(slots, own_target, mate_target, order, count, notes, alive):
    me, _, core = place()
    for side, targets in enumerate((own_target, mate_target)):
        row = me if side == 0 else me + 1 - 2 * core
        for slot in range(slots):
            index = side * slots + slot
            rows = slice(index * NOTE, (index + 1) * NOTE)
            note = jnp.full((NOTE, notes.shape[1]), targets[0, slot], jnp.int32)
            notes[rows] = note.astype(WIDE).astype(NARROW)
            live = is_live(order, count, row * slots + slot)
            alive[index : index + 1] = jnp.full((1, notes.shape[1]), live).astype(WIDE)


def write_tiles(out, products, notes, alive, tile):
    rows = products.shape[0]
    for index in range(rows // tile):
        here = slice(index * tile, (index + 1) * tile)
        kept = jnp.where(alive[index : index + 1] > 0, products[here], 0.0)
        out[here] = kept.astype(NARROW)
    out[rows:] = notes[...]


def read_targets(sent, count):
    first = sent.shape[0] - count * NOTE
    found = []
    for index in range(count):
        note = sent[first + index * NOTE : first + (index + 1) * NOTE, 0:128]
        found.append(note.astype(WIDE).astype(jnp.int32)[0, 0])
    return found


def spread(matrices, sent, tile):
    count = sent[0].shape[0] // (tile + NOTE)
    targets = [t for one in sent for t in read_targets(one, count)]
    picked = [
        jnp.concatenate(
            [m[:, pl.ds(pl.multiple_of(t * tile, tile), tile)] for t in targets], axis=1
        )
        for m in matrices
    ]
    tiles = jnp.concatenate([one[: count * tile] for one in sent], axis=0)
    return multiply(jnp.concatenate(picked, axis=0), tiles)


def pair_kernel(panels, own, mate, out):
    height = own.shape[0] // panels
    for panel in range(panels):
        rows = slice(panel * height, (panel + 1) * height)
        first = panel * CORES * height
        out[first : first + height] = own[rows]
        out[first + height : first + CORES * height] = mate[rows]


def stack_kernel(parts, *refs):
    out, first = refs[-1], 0
    for (start, size), ref in zip(parts, refs[:-1]):
        out[first : first + size] = ref[start : start + size]
        first += size


def lay_kernel(chips, *refs):
    lay_pairs(refs[-1], slice(0, refs[-1].shape[1]), refs[:-1], straight(chips), chips)


def first_kernel(tile, own, mate, notes, alive, whole, out):
    tiles = jnp.concatenate([own[...], mate[...]], axis=0)
    write_tiles(out, multiply(tiles, whole[...]), notes, alive, tile)


def ahead_kernel(chips, origins, starts, *refs):
    own, mate = refs[:2]
    pieces, out, whole = refs[2:-2], refs[-2], refs[-1]
    for piece, sources, start in zip(pieces, origins, starts):
        lay_pairs(whole, slice(0, whole.shape[1]), [piece], [sources], chips, start)
    tiles = jnp.concatenate([own[...], mate[...]], axis=0)
    out[...] = multiply(tiles, whole[...])


def next_kernel(chips, tile, *refs):
    own, mate, notes, alive, ahead = refs[:5]
    sent, rest = refs[5 : 5 + chips], refs[5 + chips :]
    past, outs = rest[: len(rest) // 2], rest[len(rest) // 2 :]
    products = ahead[...]
    products = products - spread((own, mate), sent, tile)
    out = outs[0]
    write_tiles(out, products, notes, alive, tile)
    rows = products.shape[0]
    for index, one in enumerate([*past, out] if past else []):
        outs[1][index * rows : (index + 1) * rows] = one[:rows]
    if past:
        outs[1][(len(past) + 1) * rows :] = notes[...]


def solve_kernel(chips, tile, ticks, origins, starts, *refs):
    inverse, mate = refs[:2]
    heads, (out, other, whole) = refs[2 : 2 + len(origins)], refs[-3:]
    sent = refs[2 + len(origins) : -3]
    half = PW // CORES
    height = out.shape[0]
    for piece, (tick, sources), start in zip(heads, origins, starts):
        columns = slice(tick * half, (tick + 1) * half)
        lay_pairs(whole, columns, [piece], [sources], chips, start)
    matrix = jnp.concatenate([inverse[...], mate[...]], axis=0)
    solved = multiply(matrix, whole[...])
    for tick in range(ticks):
        columns = slice(tick * half, (tick + 1) * half)
        one_tick = solved[:, columns]
        if tick:
            here = sent[(tick - 1) * chips : tick * chips]
            one_tick = one_tick - spread((inverse, mate), here, tile)
        out[:, columns] = one_tick[:height]
        other[:, columns] = one_tick[height:].astype(other.dtype)


def update_kernel(tile, ticks, count, *refs):
    sent, (out, other, total) = refs[:-3], refs[-3:]
    half = PW // CORES
    height = out.shape[0]
    _, chip, core = place()
    size = total.shape[0]
    total[...] = jnp.zeros(total.shape, total.dtype)
    block_rows = count * (ticks * tile + NOTE)
    blocks = [
        one.at[first : first + block_rows]
        for one in sent
        for first in range(0, one.shape[0], block_rows)
    ]
    for one in blocks:
        targets = read_targets(one, count)
        for index in range(ticks * count):
            tick, target = index // count, targets[index % count]
            columns = slice(tick * half, (tick + 1) * half)
            base = index * tile
            if size >= tile:
                held = size // tile
                spot = target - chip * held

                @pl.when(jnp.logical_and(spot >= 0, spot < held))
                def _(one=one, base=base, spot=spot, columns=columns):
                    rows = pl.ds(pl.multiple_of(spot * tile, tile), tile)
                    total[rows, columns] += one[base : base + tile].astype(WIDE)

            else:
                shares = tile // size
                start = base + lax.rem(chip, shares) * size

                @pl.when(target == lax.div(chip, shares))
                def _(one=one, start=start, columns=columns):
                    rows = pl.ds(pl.multiple_of(start, NOTE), size)
                    total[:, columns] += one[rows].astype(WIDE)

    out[...] = total[pl.ds(pl.multiple_of(core * height, height), height)]
    rest = total[pl.ds(pl.multiple_of((1 - core) * height, height), height)]
    other[...] = rest.astype(other.dtype)


def join_kernel(*refs):
    half = PW // CORES
    _, _, core = place()
    out, tick = refs[-1], 0
    for own, mate in zip(refs[0:-1:2], refs[1:-1:2]):
        for index in range(own.shape[1] // half):
            columns = slice(index * half, (index + 1) * half)
            for side, block in ((core, own), (1 - core, mate)):
                start = pl.multiple_of(tick * PW + side * half, half)
                out[:, pl.ds(start, half)] = block[:, columns].astype(out.dtype)
            tick += 1


def call(kernel, out_shape, args, scratch=(), weight=1):
    in_specs = [
        pl.BlockSpec(memory_space=pltpu.SMEM if a.dtype == jnp.int32 else pltpu.VMEM)
        for a in args
    ]
    return pl.pallas_call(
        kernel,
        out_shape=out_shape,
        in_specs=in_specs,
        out_specs=jax.tree.map(lambda _: pl.BlockSpec(memory_space=pltpu.VMEM), out_shape),
        scratch_shapes=list(scratch),
        compiler_params=pltpu.CompilerParams(vmem_limit_bytes=40 * 1024 * 1024),
        cost_estimate=pl.CostEstimate(flops=weight * 1000, bytes_accessed=weight, transcendentals=0),
    )(*args)


def body(
    right_side,
    entering,
    first_updates,
    diag_inverse,
    tile_blocks,
    target_row_blocks,
    tile_usage_order,
    live_tile_count,
):
    rows, chain = lax.axis_size("rows"), lax.axis_size("chain")
    chips = rows // CORES
    slots, tile, separator = tile_blocks.shape[1:]
    height = right_side.shape[0]
    ticks = right_side.shape[1] // PW
    half = PW // CORES
    inverse = diag_inverse[0]
    own = tile_blocks[0].reshape(slots * tile, separator)
    ends = (chips, chain)

    def around(block):
        return [
            hop(block, lambda core, offset=offset: offset, 0, ends) for offset in range(1, chips)
        ]

    def shape(height, width, kind):
        return jax.ShapeDtypeStruct((height, width), kind)

    is_low = lax.rem(lax.axis_index("rows"), CORES) == 0
    is_first = (lax.axis_index("chain") == 0).astype(WIDE)

    def pair_up(panels, *others):
        count = len(panels)
        split = [(one[:, :half], one[:, half:]) for one in panels]
        mine = jnp.concatenate([jnp.where(is_low, a, b) for a, b in split], axis=0)
        other = jnp.concatenate([jnp.where(is_low, b, a) for a, b in split], axis=0)
        return call(
            functools.partial(pair_kernel, count),
            shape(count * CORES * height, half, NARROW),
            (after(mine, *others) if others else mine, swap(other, rows)),
        )

    def panel(tick):
        return right_side[:, tick * PW : (tick + 1) * PW].astype(WIDE)

    head = pair_up([(panel(0) - entering).astype(NARROW)])
    heads = [head, *around(head)]
    mate = swap(own, rows)
    mate_target = swap(target_row_blocks, rows)
    mate_inverse = swap(inverse, rows)
    marks = call(
        functools.partial(mark_kernel, slots),
        (
            shape(CORES * slots * NOTE, half, NARROW),
            shape(CORES * slots, half, WIDE),
        ),
        (target_row_blocks, mate_target, tile_usage_order, live_tile_count),
    )
    rest = [
        (panel(t) - is_first * first_updates[:, (t - 1) * PW : t * PW]).astype(NARROW)
        for t in range(1, ticks)
    ]
    rest = after(pair_up(rest, marks[1]), *heads[3:])
    pair_rows = CORES * height
    origins, phases = doubling(chips)

    def phase(block, index):
        return hop(block, lambda core: phases[index][core], 0, ends)

    def stacked(parts, args, weight=1):
        rows_in_all = sum(size for _, size in parts)
        kernel = functools.partial(stack_kernel, parts)
        return call(kernel, shape(rows_in_all, half, NARROW), args, (), weight)

    begun = phase(rest, 0)

    def go_on(panel, gate):
        start = panel * pair_rows
        pieces, starts = [rest, begun], [start, start]
        if len(phases) > 1:
            held = stacked([(start, pair_rows)] * 2, (rest, after(begun, gate)))
        for index in range(1, len(phases)):
            pieces.append(phase(held, index))
            starts.append(0)
            if index + 1 < len(phases):
                size = held.shape[0]
                held = stacked([(0, size)] * 2, (held, pieces[-1]))
        return pieces, starts

    def gather(block, gate):
        held, pieces = block, [block]
        for index in range(len(phases)):
            came = phase(held, index)
            pieces.append(came)
            if index + 1 < len(phases):
                size = held.shape[0]
                held = stacked([(0, size)] * 2, (held, after(came, *gate)))
        return pieces

    block_rows = CORES * slots * (tile + NOTE)
    block = shape(block_rows, half, NARROW)
    tile_rows = CORES * slots * tile
    whole = call(
        functools.partial(lay_kernel, chips),
        shape(separator, half, NARROW),
        tuple(heads),
        (),
        LONG,
    )
    product = call(
        functools.partial(first_kernel, tile),
        block,
        (after(own, mate_inverse), mate, *marks, whole),
        (),
        LONG,
    )
    came, past, shared, laters = [], [], [], []
    for tick in range(1, ticks):
        past.append(product)
        arrived = hop(product, lambda core: 0, 1, ends)
        if tick == 1:
            arrived = stacked([(0, block_rows)], (arrived,), LONG)
        sent = [arrived, *around(arrived)]
        came += sent
        if shared:
            shared = gather(shared[0], (sent[-1],))
        if tick == 1:
            laters.append(go_on(0, product))
            laters += [go_on(panel, sent[-1]) for panel in range(1, ticks - 1)]
        pieces, starts = laters[tick - 1]
        ahead = call(
            functools.partial(ahead_kernel, chips, origins, starts),
            shape(tile_rows, half, WIDE),
            (own, mate, *pieces),
            [pltpu.VMEM((separator, half), NARROW)],
        )
        earlier = past if tick == ticks - 2 else []
        history = shape(block_rows + tick * tile_rows, half, NARROW)
        product, *history = call(
            functools.partial(next_kernel, chips, tile),
            (block, history) if earlier else (block,),
            (own, mate, *marks, ahead, *sent, *earlier),
            (),
            LITTLE if tick == 1 else SOME,
        )
        if tick == ticks - 2:
            shared = history
    last = [product, *around(product)]
    columns_of, sources, offsets = list(heads), [(0, one) for one in straight(chips)], [0] * chips
    for tick, (pieces, starts) in enumerate(laters):
        columns_of += pieces
        sources += [(tick + 1, one) for one in origins]
        offsets += starts
    mine, other = call(
        functools.partial(solve_kernel, chips, tile, ticks, sources, offsets),
        (shape(height, ticks * half, WIDE), shape(height, ticks * half, NARROW)),
        (inverse, mate_inverse, *columns_of, *came[:-1], after(came[-1], product)),
        [pltpu.VMEM((separator, ticks * half), NARROW)],
    )
    out = shape(height, ticks * PW, WIDE)
    solved = call(join_kernel, out, (mine, swap(other, rows)))

    def add_up(count, blocks, kind):
        mine, other = call(
            functools.partial(update_kernel, tile, count, CORES * slots),
            (shape(height, count * half, WIDE), shape(height, count * half, kind)),
            tuple(blocks),
            [pltpu.VMEM((CORES * height, count * half), WIDE)],
        )
        return mine, swap(other, rows)

    early = add_up(ticks - 1, [after(shared[0], product), *shared[1:]], NARROW)
    passed = (*early, *add_up(1, [after(product, early[0]), *last[1:]], WIDE))
    passed = call(join_kernel, out, passed[:-1] + (after(passed[-1], solved),))
    return solved, passed


def solution(mesh):
    placed = (
        P(("chain", "rows"), None),
        P(("chain", "rows"), None),
        P("rows", None),
        P("chain", "rows", None),
        P("chain", "rows", None, None),
        P("chain", "rows"),
        P("chain", None),
        P("chain"),
    )
    return jax.shard_map(
        body,
        mesh=mesh,
        in_specs=placed,
        out_specs=(P(("chain", "rows"), None), P(("chain", "rows"), None)),
        check_vma=False,
    )
```
